256 devices in a mesh: user: 16 (over z, core), item: 16 (over x, y).
Axes of the slice: x: 4, y: 4, z: 8, core: 2. Of those that a mesh axis runs over, the one named last changes fastest.
Arguments:
- user_emb: bfloat16 [16384, 4, 128], P(('user', 'item')), may hold values from -3 to 3
- item_emb: bfloat16 [16384, 4, 128], P(('item', 'user')), may hold values from -6 to 6
- user_gate: bfloat16 [16384, 4], P(('user', 'item')), may hold values from -48 to 48
- item_gate: bfloat16 [16384, 4], P(('item', 'user')), may hold values from -48 to 48
- positive: int32 [16384], P('user'), may hold values from 0 to 16383
- loss_weight: float32 [16384], P('user'), may hold values from 0.25 to 2
Outputs:
- user_grad: float32 [16384, 4, 128], P(('user', 'item'))
- user_gate_grad: float32 [16384, 4], P(('user', 'item'))
- item_grad: float32 [16384, 4, 128], P(('item', 'user'))
- item_gate_grad: float32 [16384, 4], P(('item', 'user'))
The draws below stay inside these ranges and needn't reach their ends.
All inputs are finite; a program needn't handle non-finite values.
Results may differ from the reference program's by a relative error of at most 0.0028.
Values may be sent and summed in bfloat16 or wider, within the bound.
No kernel may reach another device: no remote copies, remote signals or barrier semaphores. Data moves between devices by JAX's collectives and lax.ppermute only.
A program may use at most 128 MiB of HBM per device.

```python
import jax
import jax.numpy as jnp
from jax import lax

K = 4
E = 128
U_DEV = 1024
USERS = 16384
ITEMS = 16384


def shared_items(key):
    return jax.random.normal(key, (ITEMS, K, E), jnp.float32)


def draw_item_emb(key, part):
    base = shared_items(key)
    return jnp.clip(base, -6.0, 6.0).astype(jnp.bfloat16)


def draw_user_emb(key, part):
    key = jax.random.fold_in(key, 12)
    own = jnp.clip(jax.random.normal(key, (USERS, K, E), jnp.float32), -6.0, 6.0) / E ** 0.5
    signs = jax.random.randint(jax.random.fold_in(key, 21), (USERS, K, E), 0, 2).astype(jnp.float32) - 0.5
    faint = jnp.clip(jax.random.normal(jax.random.fold_in(key, 22), (USERS, K, E), jnp.float32), -4.0, 4.0) * 0.02
    place = jnp.arange(USERS) % 256
    own = jnp.where((place == 40)[:, None, None], signs, own)
    own = jnp.where((place == 168)[:, None, None], faint, own)
    return jnp.clip(own, -3.0, 3.0).astype(jnp.bfloat16)


def gate_values(key, rows):
    values = jnp.clip(jax.random.normal(key, (rows, K), jnp.float32), -4.0, 4.0) * 1.5
    return values


def draw_user_gate(key, part):
    key = jax.random.fold_in(key, 13)
    return gate_values(key, USERS).astype(jnp.bfloat16)


def draw_item_gate(key, part):
    key = jax.random.fold_in(key, 14)
    return gate_values(key, ITEMS).astype(jnp.bfloat16)


def touch_ends(values, stream_key, smallest, largest):
    longest = values.shape.index(max(values.shape))
    spots = []
    for shift in (0, 1):
        where = [jax.random.randint(jax.random.fold_in(stream_key, axis), (), 0, length) for axis, length in enumerate(values.shape)]
        where[longest] = (where[longest] + shift) % values.shape[longest]
        spots.append(tuple(where))
    return values.at[spots[0]].set(smallest).at[spots[1]].set(largest)


def levels(rng, shape, cuts, smallest, largest):
    def one(position, blocks):
        draws = jax.random.uniform(jax.random.fold_in(jax.random.fold_in(rng, 6), position), (blocks,), jnp.float32, smallest / len(cuts), largest / len(cuts))
        return jnp.repeat(jnp.exp(draws), shape[position] // blocks).reshape((-1,) + (1,) * (len(shape) - position - 1))

    loudness = one(*cuts[0])
    for cut in cuts[1:]:
        loudness = loudness * one(*cut)
    return loudness


def setup_inputs(seed: int = 0) -> dict:
    streams_of = jax.random.split(jax.random.key(seed), 7)
    user_emb = draw_user_emb(jax.random.fold_in(streams_of[6], 71), 0)
    item_emb = draw_item_emb(jax.random.fold_in(streams_of[6], 71), 0)
    user_gate = draw_user_gate(jax.random.fold_in(streams_of[6], 71), 0)
    item_gate = draw_item_gate(jax.random.fold_in(streams_of[6], 71), 0)
    positive = touch_ends(jax.random.randint(streams_of[4], (USERS,), 0, ITEMS), jax.random.fold_in(streams_of[4], 1), 0, ITEMS - 1).astype(jnp.int32)
    loss_weight = jnp.clip(0.25 + 1.75 * jax.random.uniform(streams_of[5], (USERS,), jnp.float32) ** levels(streams_of[5], (USERS,), ((0, 16),), -0.2, 0.2), 0.25, 2.0)
    return dict(user_emb=user_emb, item_emb=item_emb, user_gate=user_gate, item_gate=item_gate, positive=positive, loss_weight=loss_weight)


logit_scale = 4.0


def reference(user_emb, item_emb, user_gate, item_gate, positive, loss_weight):
    items = item_emb.astype(jnp.float32)
    igates = item_gate.astype(jnp.float32).T
    columns = jnp.arange(ITEMS, dtype=jnp.int32)
    blocks = USERS // U_DEV
    users_b = user_emb.reshape(blocks, U_DEV, K, E)
    gates_b = user_gate.reshape(blocks, U_DEV, K)
    pos_b = positive.reshape(blocks, U_DEV)
    wts_b = loss_weight.reshape(blocks, U_DEV)

    def step(carry, inputs):
        item_acc, igate_acc = carry
        u_blk, g_blk, p_blk, w_blk = inputs
        users = u_blk.astype(jnp.float32)
        scores = jnp.einsum("bke,jke->kbj", users, items, precision=lax.Precision.HIGHEST)
        gating = g_blk.astype(jnp.float32).T[:, :, None] + igates[:, None, :]
        mix = jax.nn.softmax(gating, axis=0)
        mixed = jnp.sum(mix * scores, axis=0)
        logits = logit_scale * mixed
        lse = jax.nn.logsumexp(logits, axis=1)
        hit = (columns[None, :] == p_blk[:, None]).astype(jnp.float32)
        dlogit = logit_scale * w_blk[:, None] * (jnp.exp(logits - lse[:, None]) - hit)
        share = mix * dlogit[None]
        coeff = share.astype(jnp.bfloat16).astype(jnp.float32)
        dgate = share * (scores - mixed[None])
        ugrad = jnp.einsum("kbj,jke->bke", coeff, items, precision=lax.Precision.HIGHEST)
        ggrad = jnp.sum(dgate, axis=2).T
        item_acc = item_acc + jnp.einsum("kbj,bke->jke", coeff, users, precision=lax.Precision.HIGHEST)
        igate_acc = igate_acc + jnp.sum(dgate, axis=1)
        return (item_acc, igate_acc), (ugrad, ggrad)

    init = (jnp.zeros((ITEMS, K, E), jnp.float32), jnp.zeros((K, ITEMS), jnp.float32))
    (item_grad, igate_grad), (ugrads, ggrads) = lax.scan(step, init, (users_b, gates_b, pos_b, wts_b))
    return ugrads.reshape(USERS, K, E), ggrads.reshape(USERS, K), item_grad, igate_grad.T
```

```python
import functools
import jax
import jax.numpy as jnp
from jax import lax
from jax.experimental import pallas as pl
from jax.experimental.pallas import tpu as pltpu
from jax.sharding import PartitionSpec as P

K = 4
E = 128
R = 64
CH = K * R + 16
logit_scale = 4.0
ROWS = 256
f32 = jnp.float32
bf16 = jnp.bfloat16
VM = pl.BlockSpec(memory_space=pltpu.VMEM)


def gate_factors(msg):
    g = msg[:, K * R : K * R + 8, :].astype(f32)
    rows = [g[:, k, :] for k in range(K)]
    high = jnp.maximum(jnp.maximum(rows[0], rows[1]), jnp.maximum(rows[2], rows[3]))
    low = jnp.minimum(jnp.minimum(rows[0], rows[1]), jnp.minimum(rows[2], rows[3]))
    mid = 0.5 * (high + low) + 12.0
    return [jnp.exp(r - mid) for r in rows]


def fill_user_factors(u_ref, a_ref):
    for k, rows in enumerate(gate_factors(u_ref[...])):
        cols = rows.T
        for i in range(rows.shape[0]):
            a_ref[k, i * R : (i + 1) * R, :] = jnp.broadcast_to(cols[:R, i : i + 1], (R, E))


def fill_item_factors(i_ref, b_ref):
    for k, rows in enumerate(gate_factors(i_ref[...])):
        left = lax.broadcasted_iota(jnp.int32, (8, E), 1) < R
        for p in range(rows.shape[0] // 2):
            first = jnp.broadcast_to(rows[2 * p : 2 * p + 1, :], (8, E))
            second = jnp.broadcast_to(rows[2 * p + 1 : 2 * p + 2, :], (8, E))
            b_ref[k, :, p * E : (p + 1) * E] = jnp.where(left, first, second)


def score_block(u_ref, i_ref, s_ref, blk):
    per = ROWS // R
    for k in range(K):
        u = u_ref[pl.ds(blk * per, per), k * R : (k + 1) * R, :].reshape(ROWS, E)
        it = i_ref[:, k * R : (k + 1) * R, :].reshape(-1, E)
        s_ref[k] = lax.dot_general(u, it, (((1,), (1,)), ((), ())), preferred_element_type=f32)


def tile2(x):
    return jnp.concatenate([x, x], axis=0)


def fwd_kernel(u_ref, i_ref, out_ref, a_ref, b_ref, s_ref, m_ref, t_ref):
    n = i_ref.shape[0] * R
    users = u_ref.shape[0] * R
    fill_user_factors(u_ref, a_ref)
    fill_item_factors(i_ref, b_ref)

    def block(blk, _):
        score_block(u_ref, i_ref, s_ref, blk)

        def group(r, _):
            row = blk * ROWS + r * 8
            a = [a_ref[k, pl.ds(row, 8), :] for k in range(K)]
            xs = []
            for c in range(n // E):
                lanes = slice(c * E, (c + 1) * E)
                p = [a[k] * b_ref[k, :, lanes] for k in range(K)]
                s = [s_ref[k, pl.ds(r * 8, 8), lanes] for k in range(K)]
                den = (p[0] + p[1]) + (p[2] + p[3])
                num = (p[0] * s[0] + p[1] * s[1]) + (p[2] * s[2] + p[3] * s[3])
                xs.append(logit_scale * (num * (1.0 / den)))
            top = functools.reduce(jnp.maximum, xs)
            total = functools.reduce(jnp.add, [jnp.exp(x - top) for x in xs])
            m_ref[pl.ds(row, 8), :] = top
            t_ref[pl.ds(row, 8), :] = total
            return 0

        lax.fori_loop(0, ROWS // 8, group, 0, unroll=2)
        return 0

    lax.fori_loop(0, users // ROWS, block, 0)
    for c in range(users // E):
        top = m_ref[c * E : (c + 1) * E, :].T
        total = t_ref[c * E : (c + 1) * E, :].T
        best = jnp.max(top, axis=0, keepdims=True)
        out_ref[c : c + 1, :] = best
        out_ref[8 + c : 9 + c, :] = jnp.sum(jnp.exp(top - best) * total, axis=0, keepdims=True)


def bwd_kernel(
    u_ref, i_ref, stat_ref, pos_ref, w_ref, id_ref,
    ug_ref, own_ref, other_ref,
    a_ref, b_ref, s_ref, l_ref, w4_ref, p_ref, c_ref, row_ref, col_ref, acc_ref,
):
    n = i_ref.shape[0] * R
    users = u_ref.shape[0] * R
    fill_user_factors(u_ref, a_ref)
    fill_item_factors(i_ref, b_ref)
    tops = stat_ref[:, 0:8, :]
    top = jnp.max(tops, axis=0)
    lse = top + jnp.log(jnp.sum(jnp.exp(tops - top[None]) * stat_ref[:, 8:16, :], axis=0))
    lse_t = lse.T
    w_t = (logit_scale * w_ref[...]).T
    pos_t = pos_ref[...].T
    for c in range(users // E):
        at = slice(c * E, (c + 1) * E)
        l_ref[at, :] = jnp.broadcast_to(lse_t[:, c : c + 1], (E, E))
        w4_ref[at, :] = jnp.broadcast_to(w_t[:, c : c + 1], (E, E))
        p_ref[at, :] = jnp.broadcast_to(pos_t[:, c : c + 1], (E, E))
    col_ref[...] = jnp.zeros_like(col_ref)
    acc_ref[...] = jnp.zeros_like(acc_ref)
    per = ROWS // R

    def block(blk, _):
        score_block(u_ref, i_ref, s_ref, blk)

        def group(r, _):
            row = blk * ROWS + r * 16
            rows = pl.ds(row, 16)
            a = [a_ref[k, rows, :] for k in range(K)]
            lse_r, w_r, p_r = l_ref[rows, :], w4_ref[rows, :], p_ref[rows, :]
            sums = [jnp.zeros((16, E), f32) for _ in range(K)]
            for c in range(n // E):
                lanes = slice(c * E, (c + 1) * E)
                p = [a[k] * tile2(b_ref[k, :, lanes]) for k in range(K)]
                s = [s_ref[k, pl.ds(r * 16, 16), lanes] for k in range(K)]
                inv = 1.0 / ((p[0] + p[1]) + (p[2] + p[3]))
                mixed = ((p[0] * s[0] + p[1] * s[1]) + (p[2] * s[2] + p[3] * s[3])) * inv
                prob = jnp.exp(logit_scale * mixed - lse_r)
                hit = jnp.broadcast_to(id_ref[:, lanes], (16, E)) == p_r
                dlogit = w_r * jnp.where(hit, prob - 1.0, prob)
                for k in range(K):
                    share = dlogit * (p[k] * inv)
                    c_ref[k, pl.ds(r * 16, 16), lanes] = share.astype(bf16)
                    dgate = share * (s[k] - mixed)
                    sums[k] = sums[k] + dgate
                    col_ref[k, :, lanes] += dgate[:8] + dgate[8:]
            for k in range(K):
                row_ref[k, rows, :] = sums[k]
            return 0

        lax.fori_loop(0, ROWS // 16, group, 0)
        for k in range(K):
            co = c_ref[k]
            it = i_ref[:, k * R : (k + 1) * R, :].reshape(n, E)
            u = u_ref[pl.ds(blk * per, per), k * R : (k + 1) * R, :].reshape(ROWS, E)
            ug = jnp.dot(co, it, preferred_element_type=f32)
            ug_ref[pl.ds(blk * per, per), k * R : (k + 1) * R, :] = ug.astype(bf16).reshape(per, R, E)
            if TRANS:
                acc_ref[k] += lax.dot_general(u, co, (((0,), (0,)), ((), ())), preferred_element_type=f32)
            else:
                acc_ref[k] += lax.dot_general(co, u, (((0,), (0,)), ((), ())), preferred_element_type=f32)
        return 0

    lax.fori_loop(0, users // ROWS, block, 0)

    left = lax.broadcasted_iota(jnp.int32, (1, E), 1) < R
    ug_ref[:, K * R :, :] = jnp.zeros((users // R, CH - K * R, E), bf16)
    zero = jnp.zeros((1, E), f32)
    for c in range(users // E):
        halves = ([], [])
        for k in range(K):
            total = jnp.sum(row_ref[k, c * E : (c + 1) * E, :].T, axis=0, keepdims=True)
            high = total.astype(bf16).astype(f32)
            low = total - high
            halves[0].append(jnp.where(left, high, jnp.roll(low, R, axis=1)))
            halves[1].append(jnp.where(left, jnp.roll(high, R, axis=1), low))
        for h in range(2):
            block_rows = jnp.concatenate(halves[h] + [zero] * 12, axis=0)
            ug_ref[2 * c + h, K * R :, :] = block_rows.astype(bf16)
    for half, ref in enumerate((own_ref, other_ref)):
        ref[:, K * R :, :] = jnp.zeros((ref.shape[0], 8, E), f32)
        for k in range(K):
            g = acc_ref[k].T if TRANS else acc_ref[k]
            ref[:, k * R : (k + 1) * R, :] = g[half * n // 2 : (half + 1) * n // 2].reshape(-1, R, E)
            total = jnp.sum(col_ref[k], axis=0, keepdims=True)
            for s in range(ref.shape[0] // 2):
                at = half * n // 2 + s * E
                two = total[:, at : at + E]
                ref[2 * s, K * R + k : K * R + k + 1, :] = two
                ref[2 * s + 1, K * R + k : K * R + k + 1, :] = jnp.roll(two, R, axis=1)


def add_kernel(own_ref, got_ref, *out_refs):
    left = lax.broadcasted_iota(jnp.int32, (8, E), 1) < R
    for m, ref in enumerate(out_refs):
        ref[: K * R, :] = (own_ref[m, : K * R, :] + got_ref[m, : K * R, :]).astype(bf16)
        total = own_ref[m, K * R :, :] + got_ref[m, K * R :, :]
        high = total.astype(bf16).astype(f32)
        low = total - high
        both = jnp.where(left, high, jnp.roll(low, R, axis=1))
        ref[K * R :, :] = jnp.concatenate([both, jnp.zeros_like(both)], axis=0).astype(bf16)


def final_kernel(*refs):
    z_refs, u_ref = refs[:8], refs[8]
    ug_ref, ugate_ref, ig_ref, igate_ref = refs[9:]

    def finish(get, count, out_ref, gate_ref):
        for k in range(K):
            total = get(0, k * R, R)
            for s in range(1, count):
                total = total + get(s, k * R, R)
            out_ref[:, k, :] = total
        gates = get(0, K * R, 16)
        for s in range(1, count):
            gates = gates + get(s, K * R, 16)
        gates = gates + jnp.roll(gates, R, axis=1)
        gate_ref[...] = gates.T[:R, :K]

    finish(lambda s, a, c: u_ref[s, a : a + c, :].astype(f32), u_ref.shape[0], ug_ref, ugate_ref)
    finish(lambda s, a, c: z_refs[s][a : a + c, :].astype(f32), 8, ig_ref, igate_ref)


TRANS = False
LIMIT = 56 * 1024 * 1024


def fwd(umsg, imsg):
    users, n = umsg.shape[0] * R, imsg.shape[0] * R
    return pl.pallas_call(
        fwd_kernel,
        out_shape=jax.ShapeDtypeStruct((16, E), f32),
        in_specs=[VM] * 2,
        out_specs=VM,
        scratch_shapes=[
            pltpu.VMEM((K, users, E), f32),
            pltpu.VMEM((K, 8, n), f32),
            pltpu.VMEM((K, ROWS, n), f32),
            pltpu.VMEM((users, E), f32),
            pltpu.VMEM((users, E), f32),
        ],
        compiler_params=pltpu.CompilerParams(vmem_limit_bytes=LIMIT),
        name="score_stats",
    )(umsg, imsg)


def bwd(umsg, imsg, stats, pos, w, ids):
    users, n = umsg.shape[0] * R, imsg.shape[0] * R
    half = imsg.shape[0] // 2
    part = jax.ShapeDtypeStruct((half, K * R + 8, E), f32)
    return pl.pallas_call(
        bwd_kernel,
        out_shape=(jax.ShapeDtypeStruct(umsg.shape, bf16), part, part),
        in_specs=[VM] * 6,
        out_specs=(VM, VM, VM),
        scratch_shapes=[
            pltpu.VMEM((K, users, E), f32),
            pltpu.VMEM((K, 8, n), f32),
            pltpu.VMEM((K, ROWS, n), f32),
            pltpu.VMEM((users, E), f32),
            pltpu.VMEM((users, E), f32),
            pltpu.VMEM((users, E), jnp.int32),
            pltpu.VMEM((K, ROWS, n), bf16),
            pltpu.VMEM((K, users, E), f32),
            pltpu.VMEM((K, 8, n), f32),
            pltpu.VMEM((K, E, n) if TRANS else (K, n, E), f32),
        ],
        compiler_params=pltpu.CompilerParams(vmem_limit_bytes=LIMIT),
        name="gradients",
    )(umsg, imsg, stats, pos, w, ids)


def add_halves(own, got):
    return pl.pallas_call(
        add_kernel,
        out_shape=tuple(jax.ShapeDtypeStruct((CH, E), bf16) for _ in range(8)),
        in_specs=[VM] * 2,
        out_specs=tuple([VM] * 8),
        name="add_cores",
    )(own, got)


def final(zs, us):
    return pl.pallas_call(
        final_kernel,
        out_shape=(
            jax.ShapeDtypeStruct((R, K, E), f32),
            jax.ShapeDtypeStruct((R, K), f32),
            jax.ShapeDtypeStruct((R, K, E), f32),
            jax.ShapeDtypeStruct((R, K), f32),
        ),
        in_specs=[VM] * 9,
        out_specs=(VM,) * 4,
        name="sum_parts",
    )(*zs, us)


def pack(emb, gate):
    body = jnp.transpose(emb, (1, 0, 2)).reshape(K * R, E)
    g = gate.T
    g = jnp.pad(jnp.concatenate([g, g], axis=1), ((0, 12), (0, 0)))
    return jnp.concatenate([body, g], axis=0)


def shards(user_emb, item_emb, user_gate, item_gate, positive, loss_weight):
    index = lax.axis_index("user")
    z, core = index // 2, index % 2

    def over_z(x, mask):
        return lax.ppermute(x, "user", [(2 * a + c, 2 * (a ^ mask) + c) for a in range(8) for c in range(2)])

    def swap(x):
        return lax.ppermute(x, "user", [(a, a ^ 1) for a in range(16)])

    umine, imine = pack(user_emb, user_gate), pack(item_emb, item_gate)
    own = jnp.stack([imine] + [over_z(imine, m) for m in range(1, 8)])
    umsg = lax.all_to_all(jnp.broadcast_to(umine[None], (16, CH, E)), "item", 0, 0, tiled=True)
    imsg = jnp.concatenate([own, swap(own)], axis=0)
    stats = fwd(umsg, imsg)
    stats = lax.all_to_all(jnp.broadcast_to(stats[None], (16, 16, E)), "item", 0, 0, tiled=True)
    slot = jnp.arange(16, dtype=jnp.int32)
    place = 2 * (z ^ (slot % 8)) + (core ^ (slot // 8))
    ids = lax.axis_index("item") * 1024 + place[:, None] * R + jnp.arange(R, dtype=jnp.int32)[None]
    ug, mine, other = bwd(umsg, imsg, stats, positive.reshape(8, E), loss_weight.reshape(8, E), ids.reshape(1, 1024))
    ug = lax.all_to_all(ug, "item", 0, 0, tiled=True)
    zs = add_halves(mine, swap(other))
    zs = [zs[0]] + [over_z(zs[m], m) for m in range(1, 8)]
    return final(zs, ug)


def solution(mesh):
    return jax.shard_map(
        shards,
        mesh=mesh,
        in_specs=(
            P(("user", "item"), None, None),
            P(("item", "user"), None, None),
            P(("user", "item"), None),
            P(("item", "user"), None),
            P("user"),
            P("user"),
        ),
        out_specs=(
            P(("user", "item"), None, None),
            P(("user", "item"), None),
            P(("item", "user"), None, None),
            P(("item", "user"), None),
        ),
        check_vma=False,
    )
```

```python
import functools
import jax
import jax.numpy as jnp
from jax import lax
from jax.experimental import pallas as pl
from jax.experimental.pallas import tpu as pltpu
from jax.sharding import PartitionSpec as P

K = 4
E = 128
R = 64
CH = K * R + 16
logit_scale = 4.0
ROWS = 512
f32 = jnp.float32
bf16 = jnp.bfloat16
VM = pl.BlockSpec(memory_space=pltpu.VMEM)


def gate_factors(msg):
    g = msg[:, K * R : K * R + 8, :].astype(f32)
    rows = [g[:, k, :] for k in range(K)]
    high = jnp.maximum(jnp.maximum(rows[0], rows[1]), jnp.maximum(rows[2], rows[3]))
    low = jnp.minimum(jnp.minimum(rows[0], rows[1]), jnp.minimum(rows[2], rows[3]))
    mid = 0.5 * (high + low) + 24.0
    return [jnp.exp(r - mid) for r in rows]


def fill_user_factors(u_ref, a_ref):
    for k, rows in enumerate(gate_factors(u_ref[...])):
        cols = rows.T
        for i in range(rows.shape[0]):
            a_ref[k, i * R : (i + 1) * R, :] = jnp.broadcast_to(cols[:R, i : i + 1], (R, E))


def fill_item_factors(i_ref, b_ref):
    for k, rows in enumerate(gate_factors(i_ref[...])):
        left = lax.broadcasted_iota(jnp.int32, (8, E), 1) < R
        for p in range(rows.shape[0] // 2):
            first = jnp.broadcast_to(rows[2 * p : 2 * p + 1, :], (8, E))
            second = jnp.broadcast_to(rows[2 * p + 1 : 2 * p + 2, :], (8, E))
            b_ref[k, :, p * E : (p + 1) * E] = jnp.where(left, first, second)


def tile2(x):
    return jnp.concatenate([x, x], axis=0)


def score_piece(u_ref, i_ref, s_ref, blk, k):
    per = ROWS // R
    u = u_ref[blk * per : (blk + 1) * per, pl.ds(k * R, R), :].reshape(ROWS, E)
    it = i_ref[:, pl.ds(k * R, R), :].reshape(-1, E)
    s_ref[blk % 2][k] = lax.dot_general(u, it, (((1,), (1,)), ((), ())), preferred_element_type=f32)


def inverse(x):
    y = pl.reciprocal(x, approx=True)
    return y * (2.0 - x * y)


def mixture(a, b, s):
    p = [a[k] * b[k] for k in range(K)]
    den = (p[0] + p[1]) + (p[2] + p[3])
    num = (p[0] * s[0] + p[1] * s[1]) + (p[2] * s[2] + p[3] * s[3])
    inv = inverse(den)
    return p, inv, num * inv


def fwd_kernel(u_ref, i_ref, out_ref, a_ref, b_ref, s0_ref, s1_ref, m_ref, t_ref):
    s_ref = (s0_ref, s1_ref)
    n = i_ref.shape[0] * R
    users = u_ref.shape[0] * R
    blocks = users // ROWS
    fill_user_factors(u_ref, a_ref)
    fill_item_factors(i_ref, b_ref)

    def first(r, _):
        score_piece(u_ref, i_ref, s_ref, 0, r)
        return 0

    lax.fori_loop(0, K, first, 0, unroll=4)
    for blk in range(blocks):

        def group(r, _, blk=blk):
            if blk + 1 < blocks:
                score_piece(u_ref, i_ref, s_ref, blk + 1, r)
            step = ROWS // (K)
            for h in range(step // 8):
                at = pl.multiple_of(r * step + h * 8, 8)
                rows = pl.ds(blk * ROWS + at, 8)
                a = [a_ref[k, rows, :] for k in range(K)]
                xs = []
                for c in range(n // E):
                    lanes = slice(c * E, (c + 1) * E)
                    b = [b_ref[k, :, lanes] for k in range(K)]
                    s = [s_ref[blk % 2][k, pl.ds(at, 8), lanes] for k in range(K)]
                    xs.append(SCALE2 * mixture(a, b, s)[2])
                top = functools.reduce(jnp.maximum, xs)
                m_ref[rows, :] = top
                t_ref[rows, :] = functools.reduce(jnp.add, [EXP(x - top) for x in xs])
            return 0

        lax.fori_loop(0, K, group, 0)
    for c in range(users // E):
        top = m_ref[c * E : (c + 1) * E, :].T
        total = t_ref[c * E : (c + 1) * E, :].T
        best = jnp.max(top, axis=0, keepdims=True)
        total = jnp.sum(EXP(top - best) * total, axis=0, keepdims=True)
        for d in range(out_ref.shape[0]):
            out_ref[d, c : c + 1, :] = best
            out_ref[d, 8 + c : 9 + c, :] = total


def bwd_kernel(
    u_ref, i_ref, stat_ref, pos_ref, w_ref, id_ref,
    ug_ref, own_ref, other_ref,
    a_ref, b_ref, s0_ref, s1_ref, l_ref, w4_ref, p_ref, c0_ref, c1_ref, row_ref, col_ref,
):
    s_ref, c_ref = (s0_ref, s1_ref), (c0_ref, c1_ref)
    n = i_ref.shape[0] * R
    users = u_ref.shape[0] * R
    blocks = users // ROWS
    per = ROWS // R
    fill_user_factors(u_ref, a_ref)
    fill_item_factors(i_ref, b_ref)
    tops = stat_ref[:, 0:8, :]
    top = jnp.max(tops, axis=0)
    lse = top + LOG(jnp.sum(EXP(tops - top[None]) * stat_ref[:, 8:16, :], axis=0))
    weight = logit_scale * w_ref[...]
    lse_t = (lse - LOG(weight)).T
    w_t = weight.T
    pos_t = pos_ref[...].T
    for c in range(users // E):
        at = slice(c * E, (c + 1) * E)
        l_ref[at, :] = jnp.broadcast_to(lse_t[:, c : c + 1], (E, E))
        w4_ref[at, :] = jnp.broadcast_to(w_t[:, c : c + 1], (E, E))
        p_ref[at, :] = jnp.broadcast_to(pos_t[:, c : c + 1], (E, E))
    col_ref[...] = jnp.zeros_like(col_ref)

    def gradient_piece(blk, k):
        co = c_ref[blk % 2][k]
        it = i_ref[:, pl.ds(k * R, R), :].reshape(n, E)
        u = u_ref[blk * per : (blk + 1) * per, pl.ds(k * R, R), :].reshape(ROWS, E)
        ug = jnp.dot(co, it, preferred_element_type=f32)
        ug_ref[blk * per : (blk + 1) * per, pl.ds(k * R, R), :] = ug.astype(bf16).reshape(per, R, E)
        g = lax.dot_general(co, u, (((0,), (0,)), ((), ())), preferred_element_type=f32)
        g = g.reshape(2, -1, R, E)
        for half, ref in enumerate((own_ref, other_ref)):
            if blk == 0:
                ref[:, pl.ds(k * R, R), :] = g[half]
            else:
                ref[:, pl.ds(k * R, R), :] += g[half]

    def score_only(r, _):
        score_piece(u_ref, i_ref, s_ref, 0, r)
        return 0

    def gradient_only(r, _):
        gradient_piece(blocks - 1, r)
        return 0

    lane = lax.broadcasted_iota(jnp.int32, (16, E), 1)
    lax.fori_loop(0, K, score_only, 0, unroll=4)
    for blk in range(blocks):

        def group(r, _, blk=blk):
            if blk + 1 < blocks:
                score_piece(u_ref, i_ref, s_ref, blk + 1, r)
            if blk > 0:
                gradient_piece(blk - 1, r)
            step = ROWS // (K)
            for h in range(step // 16):
                at = pl.multiple_of(r * step + h * 16, 16)
                rows = pl.ds(blk * ROWS + at, 16)
                a = [a_ref[k, rows, :] for k in range(K)]
                lse_r, w_r, p_r = l_ref[rows, :], w4_ref[rows, :], p_ref[rows, :]
                sums = [jnp.zeros((16, E), f32) for _ in range(K - 1)]
                for c in range(n // E):
                    lanes = slice(c * E, (c + 1) * E)
                    b = [tile2(b_ref[k, :, lanes]) for k in range(K)]
                    s = [s_ref[blk % 2][k, pl.ds(at, 16), lanes] for k in range(K)]
                    p, inv, mixed = mixture(a, b, s)
                    prob = EXP(SCALE2 * mixed - lse_r)
                    hit = jnp.broadcast_to(id_ref[:, lanes], (16, E)) == p_r
                    q = jnp.where(hit, prob - w_r, prob) * inv
                    for k in range(K):
                        share = q * p[k]
                        c_ref[blk % 2][k, pl.ds(at, 16), lanes] = share.astype(bf16)
                        if k < K - 1:
                            dgate = share * (s[k] - mixed)
                            sums[k] = sums[k] + dgate
                            col_ref[k, :, lanes] += dgate[:8] + dgate[8:]
                cols = [jnp.sum(x, axis=1, keepdims=True) for x in sums]
                cols.append(-(cols[0] + cols[1] + cols[2]))
                row_ref[rows, :] = jnp.where(
                    lane == 0, cols[0], jnp.where(lane == 1, cols[1], jnp.where(lane == 2, cols[2], cols[3]))
                )
            return 0

        lax.fori_loop(0, K, group, 0)
    lax.fori_loop(0, K, gradient_only, 0, unroll=4)

    left = lax.broadcasted_iota(jnp.int32, (8, E), 1) < R
    for c in range(users // E):
        total = row_ref[c * E : (c + 1) * E, :].T[0:8]
        high = total.astype(bf16).astype(f32)
        low = total - high
        first = jnp.where(left, high, jnp.roll(low, R, axis=1))
        second = jnp.where(left, jnp.roll(high, R, axis=1), low)
        for h, part in enumerate((first, second)):
            ug_ref[2 * c + h, K * R :, :] = jnp.concatenate([part, jnp.zeros_like(part)], axis=0).astype(bf16)
    totals = [jnp.sum(col_ref[k], axis=0, keepdims=True) for k in range(K - 1)]
    totals.append(-(totals[0] + totals[1] + totals[2]))
    for half, ref in enumerate((own_ref, other_ref)):
        ref[:, K * R :, :] = jnp.zeros((ref.shape[0], 8, E), f32)
        for k in range(K):
            for s in range(ref.shape[0] // 2):
                at = half * n // 2 + s * E
                two = totals[k][:, at : at + E]
                ref[2 * s, K * R + k : K * R + k + 1, :] = two
                ref[2 * s + 1, K * R + k : K * R + k + 1, :] = jnp.roll(two, R, axis=1)


def packed(emb_ref, gate_ref):
    emb = emb_ref[...].astype(f32)
    body = [emb[:, k, :].astype(bf16) for k in range(K)]
    gate = gate_ref[...].astype(f32)
    gate = jnp.concatenate([gate, gate], axis=1)
    gate = jnp.concatenate([gate, jnp.zeros((16 - K, E), f32)], axis=0)
    return jnp.concatenate(body + [gate.astype(bf16)], axis=0)


def pack_kernel(item_ref, igate_ref, user_ref, ugate_ref, iout_ref, uout_ref):
    iout_ref[...] = packed(item_ref, igate_ref)
    block = packed(user_ref, ugate_ref)
    for d in range(uout_ref.shape[0]):
        uout_ref[d] = block


def narrow(total):
    left = lax.broadcasted_iota(jnp.int32, (8, E), 1) < R
    gates = total[K * R :]
    high = gates.astype(bf16).astype(f32)
    both = jnp.where(left, high, jnp.roll(gates - high, R, axis=1))
    both = jnp.concatenate([both, jnp.zeros_like(both)], axis=0)
    return jnp.concatenate([total[: K * R].astype(bf16), both.astype(bf16)], axis=0)


def add_kernel(own_ref, got_ref, keep_ref, send_ref):
    for m in range(4):
        keep_ref[m] = own_ref[m] + got_ref[m]
        send_ref[m] = narrow(own_ref[4 + m] + got_ref[4 + m])


def join_gates(rows):
    return rows[:8] + jnp.roll(rows[:8], R, axis=1)


def widen(part):
    part = part.astype(f32)
    return jnp.concatenate([part[: K * R], join_gates(part[K * R :])], axis=0)


def pair_kernel(keep_ref, got_ref, mine_ref, *out_refs):
    mine_ref[...] = keep_ref[0] + widen(got_ref[0])
    for m, ref in enumerate(out_refs):
        ref[...] = narrow(keep_ref[m + 1] + widen(got_ref[m + 1]))


def items_kernel(mine_ref, a_ref, b_ref, c_ref, out_ref, gate_ref):
    total = mine_ref[...] + (widen(a_ref[...]) + widen(b_ref[...]) + widen(c_ref[...]))
    for k in range(K):
        out_ref[:, k, :] = total[k * R : (k + 1) * R]
    gate_ref[...] = total[K * R : K * R + K, :R]


def users_kernel(u_ref, out_ref, gate_ref):
    for k in range(K):
        total = u_ref[0, k * R : (k + 1) * R, :].astype(f32)
        for d in range(1, u_ref.shape[0]):
            total = total + u_ref[d, k * R : (k + 1) * R, :].astype(f32)
        out_ref[:, k, :] = total
    gates = u_ref[0, K * R :, :].astype(f32)
    for d in range(1, u_ref.shape[0]):
        gates = gates + u_ref[d, K * R :, :].astype(f32)
    gate_ref[...] = join_gates(gates)[:K, :R]


def call(kernel, outs, name):
    single = not isinstance(outs, tuple)

    def run(*args):
        return pl.pallas_call(
            kernel,
            out_shape=outs,
            in_specs=[VM] * len(args),
            out_specs=VM if single else (VM,) * len(outs),
            name=name,
        )(*args)

    return run


EXP, LOG, SCALE2 = jnp.exp, jnp.log, logit_scale
LIMIT = 44 * 1024 * 1024


def fwd(umsg, imsg):
    users, n = umsg.shape[0] * R, imsg.shape[0] * R
    return pl.pallas_call(
        fwd_kernel,
        out_shape=jax.ShapeDtypeStruct((16, 16, E), f32),
        in_specs=[VM] * 2,
        out_specs=VM,
        scratch_shapes=[
            pltpu.VMEM((K, users, E), f32),
            pltpu.VMEM((K, 8, n), f32),
            pltpu.VMEM((K, ROWS, n), f32),
            pltpu.VMEM((K, ROWS, n), f32),
            pltpu.VMEM((users, E), f32),
            pltpu.VMEM((users, E), f32),
        ],
        compiler_params=pltpu.CompilerParams(vmem_limit_bytes=LIMIT),
        name="score_stats",
    )(umsg, imsg)


def bwd(umsg, imsg, stats, pos, w, ids):
    users, n = umsg.shape[0] * R, imsg.shape[0] * R
    half = imsg.shape[0] // 2
    part = jax.ShapeDtypeStruct((half, K * R + 8, E), f32)
    return pl.pallas_call(
        bwd_kernel,
        out_shape=(jax.ShapeDtypeStruct(umsg.shape, bf16), part, part),
        in_specs=[VM] * 6,
        out_specs=(VM, VM, VM),
        scratch_shapes=[
            pltpu.VMEM((K, users, E), f32),
            pltpu.VMEM((K, 8, n), f32),
            pltpu.VMEM((K, ROWS, n), f32),
            pltpu.VMEM((K, ROWS, n), f32),
            pltpu.VMEM((users, E), f32),
            pltpu.VMEM((users, E), f32),
            pltpu.VMEM((users, E), jnp.int32),
            pltpu.VMEM((K, ROWS, n), bf16),
            pltpu.VMEM((K, ROWS, n), bf16),
            pltpu.VMEM((users, E), f32),
            pltpu.VMEM((K, 8, n), f32),
        ],
        compiler_params=pltpu.CompilerParams(vmem_limit_bytes=LIMIT),
        name="gradients",
    )(umsg, imsg, stats, pos, w, ids)


def shards(user_emb, item_emb, user_gate, item_gate, positive, loss_weight):
    index = lax.axis_index("user")
    z, core = index // 2, index % 2
    shape = jax.ShapeDtypeStruct

    def over_z(x, mask):
        return lax.ppermute(x, "user", [(2 * a + c, 2 * (a ^ mask) + c) for a in range(8) for c in range(2)])

    def swap(x):
        return lax.ppermute(x, "user", [(a, a ^ 1) for a in range(16)])

    mine, umsg = call(pack_kernel, (shape((CH, E), bf16), shape((16, CH, E), bf16)), "pack")(
        item_emb, item_gate.T, user_emb, user_gate.T
    )
    even = jnp.stack([mine] + [over_z(mine, m) for m in (2, 4, 6)])
    umsg = lax.all_to_all(umsg, "item", 0, 0, tiled=True)
    odd = over_z(even, 1)
    imsg = jnp.concatenate([even, odd, swap(even), swap(odd)], axis=0)
    slot = jnp.arange(16, dtype=jnp.int32)
    place = 2 * (z ^ (2 * (slot % 4) + slot // 4 % 2)) + (core ^ (slot // 8))
    ids = lax.axis_index("item") * 1024 + place[:, None] * R + jnp.arange(R, dtype=jnp.int32)[None]
    stats = fwd(umsg, imsg)
    stats = lax.all_to_all(stats, "item", 0, 0, tiled=True)
    ug, own, other = bwd(umsg, imsg, stats, positive.reshape(8, E), loss_weight.reshape(8, E), ids.reshape(1, 1024))
    grads = (shape((R, K, E), f32), shape((K, R), f32))
    got = swap(other)
    ug = lax.all_to_all(ug, "item", 0, 0, tiled=True)
    tall, one = shape((K * R + 8, E), f32), shape((CH, E), bf16)
    keep, send = call(add_kernel, (shape((4, K * R + 8, E), f32), shape((4, CH, E), bf16)), "add_cores")(own, got)
    total, *sends = call(pair_kernel, (tall, one, one, one), "add_pair")(keep, over_z(send, 1))
    parts = [over_z(x, m) for x, m in zip(sends, (2, 4, 6))]
    user_grad, user_gate_grad = call(users_kernel, grads, "sum_users")(ug)
    item_grad, item_gate_grad = call(items_kernel, grads, "sum_items")(total, *parts)
    return user_grad, user_gate_grad.T, item_grad, item_gate_grad.T


def solution(mesh):
    return jax.shard_map(
        shards,
        mesh=mesh,
        in_specs=(
            P(("user", "item"), None, None),
            P(("item", "user"), None, None),
            P(("user", "item"), None),
            P(("item", "user"), None),
            P("user"),
            P("user"),
        ),
        out_specs=(
            P(("user", "item"), None, None),
            P(("user", "item"), None),
            P(("item", "user"), None, None),
            P(("item", "user"), None),
        ),
        check_vma=False,
    )
```

```python
import functools
import jax
import jax.numpy as jnp
from jax import lax
from jax.experimental import pallas as pl
from jax.experimental.pallas import tpu as pltpu
from jax.sharding import PartitionSpec as P

K = 4
E = 128
R = 64
CH = K * R + 16
logit_scale = 4.0
ROWS = 512
f32 = jnp.float32
bf16 = jnp.bfloat16
VM = pl.BlockSpec(memory_space=pltpu.VMEM)


def gate_factors(msg):
    g = msg[:, K * R : K * R + 8, :].astype(f32)
    rows = [g[:, k, :] for k in range(K)]
    high = jnp.maximum(jnp.maximum(rows[0], rows[1]), jnp.maximum(rows[2], rows[3]))
    low = jnp.minimum(jnp.minimum(rows[0], rows[1]), jnp.minimum(rows[2], rows[3]))
    mid = 0.5 * (high + low) + 24.0
    return [jnp.exp(r - mid) for r in rows]


def fill_user_factors(u_ref, a_ref):
    for k, rows in enumerate(gate_factors(u_ref[...])):
        cols = rows.T
        for i in range(rows.shape[0]):
            a_ref[k, i * R : (i + 1) * R, :] = jnp.broadcast_to(cols[:R, i : i + 1], (R, E))


def fill_item_factors(i_ref, b_ref, start=0):
    for k, rows in enumerate(gate_factors(i_ref[...])):
        left = lax.broadcasted_iota(jnp.int32, (8, E), 1) < R
        for p in range(rows.shape[0] // 2):
            first = jnp.broadcast_to(rows[2 * p : 2 * p + 1, :], (8, E))
            second = jnp.broadcast_to(rows[2 * p + 1 : 2 * p + 2, :], (8, E))
            b_ref[k, :, start + p * E : start + (p + 1) * E] = jnp.where(left, first, second)


def tile2(x):
    return jnp.concatenate([x, x], axis=0)


def score_piece(u_ref, i_refs, s_ref, blk, k):
    per = ROWS // R
    u = u_ref[blk * per : (blk + 1) * per, pl.ds(k * R, R), :].reshape(ROWS, E)
    at = 0
    for i_ref in i_refs:
        it = i_ref[:, pl.ds(k * R, R), :].reshape(-1, E)
        s = lax.dot_general(u, it, (((1,), (1,)), ((), ())), preferred_element_type=f32)
        s_ref[blk % 2][k, :, at : at + it.shape[0]] = s
        at += it.shape[0]


def inverse(x):
    y = pl.reciprocal(x, approx=True)
    return y * (2.0 - x * y)


def mixture(a, b, s):
    p = [a[k] * b[k] for k in range(K)]
    den = (p[0] + p[1]) + (p[2] + p[3])
    num = (p[0] * s[0] + p[1] * s[1]) + (p[2] * s[2] + p[3] * s[3])
    inv = inverse(den)
    return p, inv, num * inv


def fwd_kernel(u_ref, even_ref, odd_ref, out_ref, a_ref, b_ref, s0_ref, s1_ref, m_ref, t_ref):
    s_ref, i_refs = (s0_ref, s1_ref), (even_ref, odd_ref)
    n = 2 * even_ref.shape[0] * R
    users = u_ref.shape[0] * R
    blocks = users // ROWS
    fill_user_factors(u_ref, a_ref)
    for half, i_ref in enumerate(i_refs):
        fill_item_factors(i_ref, b_ref, half * n // 2)

    def first(r, _):
        score_piece(u_ref, i_refs, s_ref, 0, r)
        return 0

    lax.fori_loop(0, K, first, 0, unroll=4)
    for blk in range(blocks):

        def group(r, _, blk=blk):
            if blk + 1 < blocks:
                score_piece(u_ref, i_refs, s_ref, blk + 1, r)
            step = ROWS // (K)
            for h in range(step // 8):
                at = pl.multiple_of(r * step + h * 8, 8)
                rows = pl.ds(blk * ROWS + at, 8)
                a = [a_ref[k, rows, :] for k in range(K)]
                xs = []
                for c in range(n // E):
                    lanes = slice(c * E, (c + 1) * E)
                    b = [b_ref[k, :, lanes] for k in range(K)]
                    s = [s_ref[blk % 2][k, pl.ds(at, 8), lanes] for k in range(K)]
                    xs.append(SCALE2 * mixture(a, b, s)[2])
                top = functools.reduce(jnp.maximum, xs)
                m_ref[rows, :] = top
                t_ref[rows, :] = functools.reduce(jnp.add, [EXP(x - top) for x in xs])
            return 0

        lax.fori_loop(0, K, group, 0)
    for c in range(users // E):
        top = m_ref[c * E : (c + 1) * E, :].T
        total = t_ref[c * E : (c + 1) * E, :].T
        best = jnp.max(top, axis=0, keepdims=True)
        total = jnp.sum(EXP(top - best) * total, axis=0, keepdims=True)
        for d in range(out_ref.shape[0]):
            out_ref[d, c : c + 1, :] = best
            out_ref[d, 8 + c : 9 + c, :] = total


def bwd_kernel(first, u_ref, i_ref, id_ref, *refs):
    if first:
        stat_ref, pos_ref, w_ref, own_ref, other_ref, ug_ref, row_ref, a_ref, l_ref, w4_ref, p_ref, *refs = refs
    else:
        a_ref, l_ref, w4_ref, p_ref, ug1_ref, row1_ref, own_ref, other_ref, ug_ref, row_ref, *refs = refs
    b_ref, s0_ref, s1_ref, c0_ref, c1_ref, col_ref = refs
    s_ref, c_ref = (s0_ref, s1_ref), (c0_ref, c1_ref)
    n = i_ref.shape[0] * R
    users = u_ref.shape[0] * R
    blocks = users // ROWS
    per = ROWS // R
    fill_item_factors(i_ref, b_ref)
    if first:
        fill_user_factors(u_ref, a_ref)
        tops = stat_ref[:, 0:8, :]
        top = jnp.max(tops, axis=0)
        lse = top + LOG(jnp.sum(EXP(tops - top[None]) * stat_ref[:, 8:16, :], axis=0))
        weight = logit_scale * w_ref[...]
        lse_t = (lse - LOG(weight)).T
        w_t = weight.T
        pos_t = pos_ref[...].T
        for c in range(users // E):
            at = slice(c * E, (c + 1) * E)
            l_ref[at, :] = jnp.broadcast_to(lse_t[:, c : c + 1], (E, E))
            w4_ref[at, :] = jnp.broadcast_to(w_t[:, c : c + 1], (E, E))
            p_ref[at, :] = jnp.broadcast_to(pos_t[:, c : c + 1], (E, E))
    col_ref[...] = jnp.zeros_like(col_ref)

    def gradient_piece(blk, k):
        co = c_ref[blk % 2][k]
        it = i_ref[:, pl.ds(k * R, R), :].reshape(n, E)
        u = u_ref[blk * per : (blk + 1) * per, pl.ds(k * R, R), :].reshape(ROWS, E)
        at = (slice(blk * per, (blk + 1) * per), pl.ds(k * R, R))
        ug = jnp.dot(co, it, preferred_element_type=f32).reshape(per, R, E)
        ug_ref[at] = ug if first else (ug + ug1_ref[at]).astype(bf16)
        g = lax.dot_general(co, u, (((0,), (0,)), ((), ())), preferred_element_type=f32)
        g = g.reshape(2, -1, R, E)
        for half, ref in enumerate((own_ref, other_ref)):
            if blk == 0:
                ref[:, pl.ds(k * R, R), :] = g[half]
            else:
                ref[:, pl.ds(k * R, R), :] += g[half]

    def score_only(r, _):
        score_piece(u_ref, (i_ref,), s_ref, 0, r)
        return 0

    def gradient_only(r, _):
        gradient_piece(blocks - 1, r)
        return 0

    lane = lax.broadcasted_iota(jnp.int32, (16, E), 1)
    lax.fori_loop(0, K, score_only, 0, unroll=4)
    for blk in range(blocks):

        def group(r, _, blk=blk):
            if blk + 1 < blocks:
                score_piece(u_ref, (i_ref,), s_ref, blk + 1, r)
            if blk > 0:
                gradient_piece(blk - 1, r)
            step = ROWS // K
            for h in range(step // 16):
                at = pl.multiple_of(r * step + h * 16, 16)
                rows = pl.ds(blk * ROWS + at, 16)
                a = [a_ref[k, rows, :] for k in range(K)]
                lse_r, w_r, p_r = l_ref[rows, :], w4_ref[rows, :], p_ref[rows, :]
                sums = [jnp.zeros((16, E), f32) for _ in range(K - 1)]
                for c in range(n // E):
                    lanes = slice(c * E, (c + 1) * E)
                    b = [tile2(b_ref[k, :, lanes]) for k in range(K)]
                    s = [s_ref[blk % 2][k, pl.ds(at, 16), lanes] for k in range(K)]
                    p, inv, mixed = mixture(a, b, s)
                    prob = EXP(SCALE2 * mixed - lse_r)
                    hit = jnp.broadcast_to(id_ref[:, lanes], (16, E)) == p_r
                    q = jnp.where(hit, prob - w_r, prob) * inv
                    for k in range(K):
                        share = q * p[k]
                        c_ref[blk % 2][k, pl.ds(at, 16), lanes] = share.astype(bf16)
                        if k < K - 1:
                            dgate = share * (s[k] - mixed)
                            sums[k] = sums[k] + dgate
                            col_ref[k, :, lanes] += dgate[:8] + dgate[8:]
                cols = [jnp.sum(x, axis=1, keepdims=True) for x in sums]
                cols.append(-(cols[0] + cols[1] + cols[2]))
                both = jnp.where(
                    lane == 0, cols[0], jnp.where(lane == 1, cols[1], jnp.where(lane == 2, cols[2], cols[3]))
                )
                row_ref[rows, :] = both if first else both + row1_ref[rows, :]
            return 0

        lax.fori_loop(0, K, group, 0)
    lax.fori_loop(0, K, gradient_only, 0, unroll=4)

    if not first:
        left = lax.broadcasted_iota(jnp.int32, (8, E), 1) < R
        for c in range(users // E):
            total = row_ref[c * E : (c + 1) * E, :].T[0:8]
            high = total.astype(bf16).astype(f32)
            low = total - high
            halves = jnp.where(left, high, jnp.roll(low, R, axis=1)), jnp.where(left, jnp.roll(high, R, axis=1), low)
            for h, part in enumerate(halves):
                ug_ref[2 * c + h, K * R :, :] = jnp.concatenate([part, jnp.zeros_like(part)], axis=0).astype(bf16)
    totals = [jnp.sum(col_ref[k], axis=0, keepdims=True) for k in range(K - 1)]
    totals.append(-(totals[0] + totals[1] + totals[2]))
    for half, ref in enumerate((own_ref, other_ref)):
        ref[:, K * R :, :] = jnp.zeros((ref.shape[0], 8, E), f32)
        for k in range(K):
            for s in range(ref.shape[0] // 2):
                at = half * n // 2 + s * E
                two = totals[k][:, at : at + E]
                ref[2 * s, K * R + k : K * R + k + 1, :] = two
                ref[2 * s + 1, K * R + k : K * R + k + 1, :] = jnp.roll(two, R, axis=1)


def packed(emb_ref, gate_ref):
    emb = emb_ref[...].astype(f32)
    body = [emb[:, k, :].astype(bf16) for k in range(K)]
    gate = gate_ref[...].astype(f32)
    gate = jnp.concatenate([gate, gate], axis=1)
    gate = jnp.concatenate([gate, jnp.zeros((16 - K, E), f32)], axis=0)
    return jnp.concatenate(body + [gate.astype(bf16)], axis=0)


def pack_kernel(item_ref, igate_ref, user_ref, ugate_ref, iout_ref, uout_ref):
    iout_ref[...] = packed(item_ref, igate_ref)
    block = packed(user_ref, ugate_ref)
    for d in range(uout_ref.shape[0]):
        uout_ref[d] = block


def narrow(total):
    left = lax.broadcasted_iota(jnp.int32, (8, E), 1) < R
    gates = total[K * R :]
    high = gates.astype(bf16).astype(f32)
    both = jnp.where(left, high, jnp.roll(gates - high, R, axis=1))
    both = jnp.concatenate([both, jnp.zeros_like(both)], axis=0)
    return jnp.concatenate([total[: K * R].astype(bf16), both.astype(bf16)], axis=0)


def add_kernel(own_ref, got_ref, send_ref):
    for m in range(send_ref.shape[0]):
        send_ref[m] = narrow(own_ref[m] + got_ref[m])


def join_gates(rows):
    return rows[:8] + jnp.roll(rows[:8], R, axis=1)


def widen(part):
    part = part.astype(f32)
    return jnp.concatenate([part[: K * R], join_gates(part[K * R :])], axis=0)


def pair_kernel(own_ref, got_ref, part_ref, mine_ref, *out_refs):
    mine_ref[...] = own_ref[0] + got_ref[0] + widen(part_ref[0])
    for m, ref in enumerate(out_refs):
        ref[...] = narrow(own_ref[m + 1] + got_ref[m + 1] + widen(part_ref[m + 1]))


def items_kernel(mine_ref, a_ref, b_ref, c_ref, out_ref, gate_ref):
    total = mine_ref[...] + (widen(a_ref[...]) + widen(b_ref[...]) + widen(c_ref[...]))
    for k in range(K):
        out_ref[:, k, :] = total[k * R : (k + 1) * R]
    gate_ref[...] = total[K * R : K * R + K, :R]


def users_kernel(u_ref, out_ref, gate_ref):
    for k in range(K):
        total = u_ref[0, k * R : (k + 1) * R, :].astype(f32)
        for d in range(1, u_ref.shape[0]):
            total = total + u_ref[d, k * R : (k + 1) * R, :].astype(f32)
        out_ref[:, k, :] = total
    gates = u_ref[0, K * R :, :].astype(f32)
    for d in range(1, u_ref.shape[0]):
        gates = gates + u_ref[d, K * R :, :].astype(f32)
    gate_ref[...] = join_gates(gates)[:K, :R]


def estimate(micros):
    return pl.CostEstimate(flops=micros * 10**9, transcendentals=0, bytes_accessed=micros * 3 * 10**6)


def call(kernel, outs, name, limit=8 * 1024 * 1024):
    single = not isinstance(outs, tuple)

    def run(*args):
        return pl.pallas_call(
            kernel,
            out_shape=outs,
            in_specs=[VM] * len(args),
            out_specs=VM if single else (VM,) * len(outs),
            cost_estimate=estimate(2),
            compiler_params=pltpu.CompilerParams(vmem_limit_bytes=limit),
            name=name,
        )(*args)

    return run


EXP, LOG, SCALE2 = jnp.exp, jnp.log, logit_scale
LIMIT = 44 * 1024 * 1024
LIMIT2 = 28 * 1024 * 1024


def fwd(umsg, even, odd):
    users, n = umsg.shape[0] * R, 2 * even.shape[0] * R
    return pl.pallas_call(
        fwd_kernel,
        out_shape=jax.ShapeDtypeStruct((16, 16, E), f32),
        in_specs=[VM] * 3,
        out_specs=VM,
        scratch_shapes=[
            pltpu.VMEM((K, users, E), f32),
            pltpu.VMEM((K, 8, n), f32),
            pltpu.VMEM((K, ROWS, n), f32),
            pltpu.VMEM((K, ROWS, n), f32),
            pltpu.VMEM((users, E), f32),
            pltpu.VMEM((users, E), f32),
        ],
        compiler_params=pltpu.CompilerParams(vmem_limit_bytes=LIMIT),
        cost_estimate=estimate(6),
        name="score_stats",
    )(umsg, even, odd)


def bwd(first, umsg, imsg, ids, *more):
    users, n = umsg.shape[0] * R, imsg.shape[0] * R
    shape = jax.ShapeDtypeStruct
    part = shape((imsg.shape[0] // 2, K * R + 8, E), f32)
    column = shape((users, E), f32)
    outs = [part, part]
    if first:
        outs += [shape((users // R, K * R, E), f32), column, shape((K, users, E), f32)]
        outs += [column, column, shape((users, E), jnp.int32)]
    else:
        outs += [shape(umsg.shape, bf16)]
    return pl.pallas_call(
        functools.partial(bwd_kernel, first),
        out_shape=tuple(outs),
        in_specs=[VM] * (3 + len(more)),
        out_specs=(VM,) * len(outs),
        scratch_shapes=([] if first else [pltpu.VMEM((users, E), f32)])
        + [
            pltpu.VMEM((K, 8, n), f32),
            pltpu.VMEM((K, ROWS, n), f32),
            pltpu.VMEM((K, ROWS, n), f32),
            pltpu.VMEM((K, ROWS, n), bf16),
            pltpu.VMEM((K, ROWS, n), bf16),
            pltpu.VMEM((K, 8, n), f32),
        ],
        compiler_params=pltpu.CompilerParams(vmem_limit_bytes=LIMIT2),
        cost_estimate=estimate(8),
        name="gradients_odd" if first else "gradients_even",
    )(umsg, imsg, ids, *more)


def shards(user_emb, item_emb, user_gate, item_gate, positive, loss_weight):
    index = lax.axis_index("user")
    z, core = index // 2, index % 2
    shape = jax.ShapeDtypeStruct

    def over_z(x, mask):
        return lax.ppermute(x, "user", [(2 * a + c, 2 * (a ^ mask) + c) for a in range(8) for c in range(2)])

    def swap(x):
        return lax.ppermute(x, "user", [(a, a ^ 1) for a in range(16)])

    packs = (shape((CH, E), bf16), shape((16, CH, E), bf16))
    mine, umsg = call(pack_kernel, packs, "pack", 60 * 1024 * 1024)(item_emb, item_gate.T, user_emb, user_gate.T)
    umsg = lax.all_to_all(umsg, "item", 0, 0, tiled=True)
    far = over_z(mine, 4)
    mine, far = lax.optimization_barrier((mine, far))
    even = jnp.stack([mine, over_z(mine, 2), far, over_z(mine, 6)])
    odd = over_z(even, 1)
    even = jnp.concatenate([even, swap(even)], axis=0)
    odd = jnp.concatenate([odd, swap(odd)], axis=0)
    slot = jnp.arange(8, dtype=jnp.int32)

    def ids(parity):
        place = 2 * (z ^ (2 * (slot % 4) + parity)) + (core ^ (slot // 4))
        place = lax.axis_index("item") * 1024 + place[:, None] * R + jnp.arange(R, dtype=jnp.int32)[None]
        return place.reshape(1, 512)

    stats = lax.all_to_all(fwd(umsg, even, odd), "item", 0, 0, tiled=True)
    own1, other1, ug1, row1, *kept = bwd(
        True, umsg, odd, ids(1), stats, positive.reshape(8, E), loss_weight.reshape(8, E)
    )
    got1 = swap(other1)
    own0, other0, ug = bwd(False, umsg, even, ids(0), *kept, ug1, row1)
    got0 = swap(other0)
    send = call(add_kernel, shape((4, CH, E), bf16), "add_cores")(own1, got1)
    ug, send = lax.optimization_barrier((ug, send))
    ug = lax.all_to_all(ug, "item", 0, 0, tiled=True)
    tall, one = shape((K * R + 8, E), f32), shape((CH, E), bf16)
    grads = (shape((R, K, E), f32), shape((K, R), f32))
    total, *sends = call(pair_kernel, (tall, one, one, one), "add_pair")(own0, got0, over_z(send, 1))
    parts = [over_z(x, m) for x, m in zip(sends, (2, 4, 6))]
    user_grad, user_gate_grad = call(users_kernel, grads, "sum_users")(ug)
    item_grad, item_gate_grad = call(items_kernel, grads, "sum_items")(total, *parts)
    return user_grad, user_gate_grad.T, item_grad, item_gate_grad.T


def solution(mesh):
    return jax.shard_map(
        shards,
        mesh=mesh,
        in_specs=(
            P(("user", "item"), None, None),
            P(("item", "user"), None, None),
            P(("user", "item"), None),
            P(("item", "user"), None),
            P("user"),
            P("user"),
        ),
        out_specs=(
            P(("user", "item"), None, None),
            P(("user", "item"), None),
            P(("item", "user"), None, None),
            P(("item", "user"), None),
        ),
        check_vma=False,
    )
```

```python
import functools
import jax
import jax.numpy as jnp
from jax import lax
from jax.experimental import pallas as pl
from jax.experimental.pallas import tpu as pltpu
from jax.sharding import PartitionSpec as P

K = 4
E = 128
R = 64
CH = K * R + 16
logit_scale = 4.0
ROWS = 512
BROWS = 512
f32 = jnp.float32
bf16 = jnp.bfloat16
VM = pl.BlockSpec(memory_space=pltpu.VMEM)


def gate_factors(msg):
    g = msg[:, K * R : K * R + 8, :].astype(f32)
    rows = [g[:, k, :] for k in range(K)]
    high = jnp.maximum(jnp.maximum(rows[0], rows[1]), jnp.maximum(rows[2], rows[3]))
    low = jnp.minimum(jnp.minimum(rows[0], rows[1]), jnp.minimum(rows[2], rows[3]))
    mid = 0.5 * (high + low) + 24.0
    return [jnp.exp(r - mid) for r in rows]


def fill_user_factors(u_ref, a_ref):
    for k, rows in enumerate(gate_factors(u_ref[...])):
        cols = rows.T
        for i in range(rows.shape[0]):
            a_ref[k, i * R : (i + 1) * R, :] = jnp.broadcast_to(cols[:R, i : i + 1], (R, E))


def fill_item_factors(i_ref, b_ref, start=0):
    for k, rows in enumerate(gate_factors(i_ref[...])):
        left = lax.broadcasted_iota(jnp.int32, (8, E), 1) < R
        for p in range(rows.shape[0] // 2):
            first = jnp.broadcast_to(rows[2 * p : 2 * p + 1, :], (8, E))
            second = jnp.broadcast_to(rows[2 * p + 1 : 2 * p + 2, :], (8, E))
            b_ref[k, :, start + p * E : start + (p + 1) * E] = jnp.where(left, first, second)


def tile2(x):
    return jnp.concatenate([x, x], axis=0)


def score_piece(u_ref, i_refs, s_ref, blk, k):
    rows = s_ref[0].shape[1]
    per = rows // R
    u = u_ref[blk * per : (blk + 1) * per, pl.ds(k * R, R), :].reshape(rows, E)
    at = 0
    for i_ref in i_refs:
        it = i_ref[:, pl.ds(k * R, R), :].reshape(-1, E)
        s = lax.dot_general(u, it, (((1,), (1,)), ((), ())), preferred_element_type=f32)
        s_ref[blk % 2][k, :, at : at + it.shape[0]] = s
        at += it.shape[0]


def inverse(x):
    y = pl.reciprocal(x, approx=True)
    return y * (2.0 - x * y)


def mixture(a, b, s):
    p = [a[k] * b[k] for k in range(K)]
    den = (p[0] + p[1]) + (p[2] + p[3])
    num = (p[0] * s[0] + p[1] * s[1]) + (p[2] * s[2] + p[3] * s[3])
    inv = inverse(den)
    return p, inv, num * inv


def fwd_kernel(u_ref, even_ref, odd_ref, out_ref, a_ref, b_ref, s0_ref, s1_ref, m_ref, t_ref):
    s_ref, i_refs = (s0_ref, s1_ref), (even_ref, odd_ref)
    n = 2 * even_ref.shape[0] * R
    users = u_ref.shape[0] * R
    blocks = users // ROWS
    fill_user_factors(u_ref, a_ref)
    for half, i_ref in enumerate(i_refs):
        fill_item_factors(i_ref, b_ref, half * n // 2)

    def first(r, _):
        score_piece(u_ref, i_refs, s_ref, 0, r)
        return 0

    lax.fori_loop(0, K, first, 0, unroll=4)
    for blk in range(blocks):

        def group(r, _, blk=blk):
            if blk + 1 < blocks:
                score_piece(u_ref, i_refs, s_ref, blk + 1, r)
            step = ROWS // (K)
            for h in range(step // 8):
                at = r * step + h * 8
                rows = pl.ds(blk * ROWS + at, 8)
                a = [a_ref[k, rows, :] for k in range(K)]
                xs = []
                for c in range(n // E):
                    lanes = slice(c * E, (c + 1) * E)
                    b = [b_ref[k, :, lanes] for k in range(K)]
                    s = [s_ref[blk % 2][k, pl.ds(at, 8), lanes] for k in range(K)]
                    xs.append(SCALE2 * mixture(a, b, s)[2])
                top = functools.reduce(jnp.maximum, xs)
                m_ref[rows, :] = top
                t_ref[rows, :] = functools.reduce(jnp.add, [EXP(x - top) for x in xs])
            return 0

        lax.fori_loop(0, K, group, 0)
    for c in range(users // E):
        top = m_ref[c * E : (c + 1) * E, :].T
        total = t_ref[c * E : (c + 1) * E, :].T
        best = jnp.max(top, axis=0, keepdims=True)
        total = jnp.sum(EXP(top - best) * total, axis=0, keepdims=True)
        for d in range(out_ref.shape[0]):
            out_ref[d, c : c + 1, :] = best
            out_ref[d, 8 + c : 9 + c, :] = total


def bwd_kernel(first, u_ref, i_ref, id_ref, *refs):
    if first:
        stat_ref, pos_ref, w_ref, own_ref, other_ref, ug_ref, row_ref, a_ref, l_ref, w4_ref, p_ref, *refs = refs
    else:
        a_ref, l_ref, w4_ref, p_ref, ug1_ref, row1_ref, own_ref, other_ref, ug_ref, row_ref, *refs = refs
    b_ref, s0_ref, s1_ref, c0_ref, c1_ref, col_ref = refs
    s_ref, c_ref = (s0_ref, s1_ref), (c0_ref, c1_ref)
    n = i_ref.shape[0] * R
    users = u_ref.shape[0] * R
    blocks = users // BROWS
    per = BROWS // R
    fill_item_factors(i_ref, b_ref)
    if first:
        fill_user_factors(u_ref, a_ref)
        tops = stat_ref[:, 0:8, :]
        top = jnp.max(tops, axis=0)
        lse = top + LOG(jnp.sum(EXP(tops - top[None]) * stat_ref[:, 8:16, :], axis=0))
        weight = logit_scale * w_ref[...]
        lse_t = (lse - LOG(weight)).T
        w_t = weight.T
        pos_t = pos_ref[...].T
        for c in range(users // E):
            at = slice(c * E, (c + 1) * E)
            l_ref[at, :] = jnp.broadcast_to(lse_t[:, c : c + 1], (E, E))
            w4_ref[at, :] = jnp.broadcast_to(w_t[:, c : c + 1], (E, E))
            p_ref[at, :] = jnp.broadcast_to(pos_t[:, c : c + 1], (E, E))
    col_ref[...] = jnp.zeros_like(col_ref)

    def gradient_piece(blk, k):
        co = c_ref[blk % 2][k]
        it = i_ref[:, pl.ds(k * R, R), :].reshape(n, E)
        u = u_ref[blk * per : (blk + 1) * per, pl.ds(k * R, R), :].reshape(BROWS, E)
        at = (slice(blk * per, (blk + 1) * per), pl.ds(k * R, R))
        ug = jnp.dot(co, it, preferred_element_type=f32).reshape(per, R, E)
        ug_ref[at] = ug if first else (ug + ug1_ref[at]).astype(bf16)
        g = lax.dot_general(co, u, (((0,), (0,)), ((), ())), preferred_element_type=f32)
        g = g.reshape(2, -1, R, E)
        for half, ref in enumerate((own_ref, other_ref)):
            if blk == 0:
                ref[:, pl.ds(k * R, R), :] = g[half]
            else:
                ref[:, pl.ds(k * R, R), :] += g[half]

    def score_only(r, _):
        score_piece(u_ref, (i_ref,), s_ref, 0, r)
        return 0

    def gradient_only(r, _):
        gradient_piece(blocks - 1, r)
        return 0

    lane = lax.broadcasted_iota(jnp.int32, (16, E), 1)
    lax.fori_loop(0, K, score_only, 0, unroll=4)
    for blk in range(blocks):

        def group(r, _, blk=blk):
            if blk + 1 < blocks:
                score_piece(u_ref, (i_ref,), s_ref, blk + 1, r)
            if blk > 0:
                gradient_piece(blk - 1, r)
            step = BROWS // K
            for h in range(step // 16):
                at = r * step + h * 16
                rows = pl.ds(blk * BROWS + at, 16)
                a = [a_ref[k, rows, :] for k in range(K)]
                lse_r, w_r, p_r = l_ref[rows, :], w4_ref[rows, :], p_ref[rows, :]
                sums = [jnp.zeros((16, E), f32) for _ in range(K - 1)]
                for c in range(n // E):
                    lanes = slice(c * E, (c + 1) * E)
                    b = [tile2(b_ref[k, :, lanes]) for k in range(K)]
                    s = [s_ref[blk % 2][k, pl.ds(at, 16), lanes] for k in range(K)]
                    p, inv, mixed = mixture(a, b, s)
                    prob = EXP(SCALE2 * mixed - lse_r)
                    hit = jnp.broadcast_to(id_ref[:, lanes], (16, E)) == p_r
                    q = jnp.where(hit, prob - w_r, prob) * inv
                    for k in range(K):
                        share = q * p[k]
                        c_ref[blk % 2][k, pl.ds(at, 16), lanes] = share.astype(bf16)
                        if k < K - 1:
                            dgate = share * (s[k] - mixed)
                            sums[k] = sums[k] + dgate
                            col_ref[k, :, lanes] += dgate[:8] + dgate[8:]
                cols = [jnp.sum(x, axis=1, keepdims=True) for x in sums]
                cols.append(-(cols[0] + cols[1] + cols[2]))
                both = jnp.where(
                    lane == 0, cols[0], jnp.where(lane == 1, cols[1], jnp.where(lane == 2, cols[2], cols[3]))
                )
                row_ref[rows, :] = both if first else both + row1_ref[rows, :]
            return 0

        for r in range(K):
            group(r, 0)
    lax.fori_loop(0, K, gradient_only, 0, unroll=4)

    if not first:
        left = lax.broadcasted_iota(jnp.int32, (8, E), 1) < R
        for c in range(users // E):
            total = row_ref[c * E : (c + 1) * E, :].T[0:8]
            high = total.astype(bf16).astype(f32)
            low = total - high
            halves = jnp.where(left, high, jnp.roll(low, R, axis=1)), jnp.where(left, jnp.roll(high, R, axis=1), low)
            for h, part in enumerate(halves):
                ug_ref[2 * c + h, K * R :, :] = jnp.concatenate([part, jnp.zeros_like(part)], axis=0).astype(bf16)
    totals = [jnp.sum(col_ref[k], axis=0, keepdims=True) for k in range(K - 1)]
    totals.append(-(totals[0] + totals[1] + totals[2]))
    for half, ref in enumerate((own_ref, other_ref)):
        ref[:, K * R :, :] = jnp.zeros((ref.shape[0], 8, E), f32)
        for k in range(K):
            for s in range(ref.shape[0] // 2):
                at = half * n // 2 + s * E
                two = totals[k][:, at : at + E]
                ref[2 * s, K * R + k : K * R + k + 1, :] = two
                ref[2 * s + 1, K * R + k : K * R + k + 1, :] = jnp.roll(two, R, axis=1)


def packed(emb_ref, gate_ref):
    emb = emb_ref[...].astype(f32)
    body = [emb[:, k, :].astype(bf16) for k in range(K)]
    gate = gate_ref[...].astype(f32)
    gate = jnp.concatenate([gate, gate], axis=1)
    gate = jnp.concatenate([gate, jnp.zeros((16 - K, E), f32)], axis=0)
    return jnp.concatenate(body + [gate.astype(bf16)], axis=0)


def pack_kernel(item_ref, igate_ref, user_ref, ugate_ref, iout_ref, uout_ref):
    iout_ref[...] = packed(item_ref, igate_ref)
    block = packed(user_ref, ugate_ref)
    for d in range(uout_ref.shape[0]):
        uout_ref[d] = block


def narrow(total):
    left = lax.broadcasted_iota(jnp.int32, (8, E), 1) < R
    gates = total[K * R :]
    high = gates.astype(bf16).astype(f32)
    both = jnp.where(left, high, jnp.roll(gates - high, R, axis=1))
    both = jnp.concatenate([both, jnp.zeros_like(both)], axis=0)
    return jnp.concatenate([total[: K * R].astype(bf16), both.astype(bf16)], axis=0)


def add_kernel(own_ref, got_ref, send_ref):
    for m in range(send_ref.shape[0]):
        send_ref[m] = narrow(own_ref[m] + got_ref[m])


def join_gates(rows):
    return rows[:8] + jnp.roll(rows[:8], R, axis=1)


def widen(part):
    part = part.astype(f32)
    return jnp.concatenate([part[: K * R], join_gates(part[K * R :])], axis=0)


def pair_kernel(own_ref, got_ref, part_ref, mine_ref, *out_refs):
    mine_ref[...] = own_ref[0] + got_ref[0] + widen(part_ref[0])
    for m, ref in enumerate(out_refs):
        ref[...] = narrow(own_ref[m + 1] + got_ref[m + 1] + widen(part_ref[m + 1]))


def items_kernel(mine_ref, a_ref, b_ref, c_ref, out_ref, gate_ref):
    total = mine_ref[...] + (widen(a_ref[...]) + widen(b_ref[...]) + widen(c_ref[...]))
    for k in range(K):
        out_ref[:, k, :] = total[k * R : (k + 1) * R]
    gate_ref[...] = total[K * R : K * R + K, :R]


def users_kernel(u_ref, out_ref, gate_ref):
    for k in range(K):
        total = u_ref[0, k * R : (k + 1) * R, :].astype(f32)
        for d in range(1, u_ref.shape[0]):
            total = total + u_ref[d, k * R : (k + 1) * R, :].astype(f32)
        out_ref[:, k, :] = total
    gates = u_ref[0, K * R :, :].astype(f32)
    for d in range(1, u_ref.shape[0]):
        gates = gates + u_ref[d, K * R :, :].astype(f32)
    gate_ref[...] = join_gates(gates)[:K, :R]


def estimate(micros):
    return pl.CostEstimate(flops=micros * 10**9, transcendentals=0, bytes_accessed=micros * 3 * 10**6)


def call(kernel, outs, name, limit=8 * 1024 * 1024):
    single = not isinstance(outs, tuple)

    def run(*args):
        return pl.pallas_call(
            kernel,
            out_shape=outs,
            in_specs=[VM] * len(args),
            out_specs=VM if single else (VM,) * len(outs),
            cost_estimate=estimate(2),
            compiler_params=pltpu.CompilerParams(vmem_limit_bytes=limit),
            name=name,
        )(*args)

    return run


EXP, LOG, SCALE2 = jnp.exp, jnp.log, logit_scale
LIMIT = 44 * 1024 * 1024
LIMIT2 = 44 * 1024 * 1024


def fwd(umsg, even, odd):
    users, n = umsg.shape[0] * R, 2 * even.shape[0] * R
    return pl.pallas_call(
        fwd_kernel,
        out_shape=jax.ShapeDtypeStruct((16, 16, E), f32),
        in_specs=[VM] * 3,
        out_specs=VM,
        scratch_shapes=[
            pltpu.VMEM((K, users, E), f32),
            pltpu.VMEM((K, 8, n), f32),
            pltpu.VMEM((K, ROWS, n), f32),
            pltpu.VMEM((K, ROWS, n), f32),
            pltpu.VMEM((users, E), f32),
            pltpu.VMEM((users, E), f32),
        ],
        compiler_params=pltpu.CompilerParams(vmem_limit_bytes=LIMIT),
        cost_estimate=estimate(6),
        name="score_stats",
    )(umsg, even, odd)


def bwd(first, umsg, imsg, ids, *more):
    users, n = umsg.shape[0] * R, imsg.shape[0] * R
    shape = jax.ShapeDtypeStruct
    part = shape((imsg.shape[0] // 2, K * R + 8, E), f32)
    column = shape((users, E), f32)
    outs = [part, part]
    if first:
        outs += [shape((users // R, K * R, E), f32), column, shape((K, users, E), f32)]
        outs += [column, column, shape((users, E), jnp.int32)]
    else:
        outs += [shape(umsg.shape, bf16)]
    return pl.pallas_call(
        functools.partial(bwd_kernel, first),
        out_shape=tuple(outs),
        in_specs=[VM] * (3 + len(more)),
        out_specs=(VM,) * len(outs),
        scratch_shapes=([] if first else [pltpu.VMEM((users, E), f32)])
        + [
            pltpu.VMEM((K, 8, n), f32),
            pltpu.VMEM((K, BROWS, n), f32),
            pltpu.VMEM((K, BROWS, n), f32),
            pltpu.VMEM((K, BROWS, n), bf16),
            pltpu.VMEM((K, BROWS, n), bf16),
            pltpu.VMEM((K, 8, n), f32),
        ],
        compiler_params=pltpu.CompilerParams(vmem_limit_bytes=LIMIT2),
        cost_estimate=estimate(8),
        name="gradients_odd" if first else "gradients_even",
    )(umsg, imsg, ids, *more)


def shards(user_emb, item_emb, user_gate, item_gate, positive, loss_weight):
    index = lax.axis_index("user")
    z, core = index // 2, index % 2
    shape = jax.ShapeDtypeStruct

    def over_z(x, mask):
        return lax.ppermute(x, "user", [(2 * a + c, 2 * (a ^ mask) + c) for a in range(8) for c in range(2)])

    def swap(x):
        return lax.ppermute(x, "user", [(a, a ^ 1) for a in range(16)])

    packs = (shape((CH, E), bf16), shape((16, CH, E), bf16))
    mine, umsg = call(pack_kernel, packs, "pack", 60 * 1024 * 1024)(item_emb, item_gate.T, user_emb, user_gate.T)
    umsg = lax.all_to_all(umsg, "item", 0, 0, tiled=True)
    far = over_z(mine, 4)
    mine, far = lax.optimization_barrier((mine, far))
    even = jnp.stack([mine, over_z(mine, 2), far, over_z(mine, 6)])
    odd = over_z(even, 1)
    even = jnp.concatenate([even, swap(even)], axis=0)
    odd = jnp.concatenate([odd, swap(odd)], axis=0)
    slot = jnp.arange(8, dtype=jnp.int32)

    def ids(parity):
        place = 2 * (z ^ (2 * (slot % 4) + parity)) + (core ^ (slot // 4))
        place = lax.axis_index("item") * 1024 + place[:, None] * R + jnp.arange(R, dtype=jnp.int32)[None]
        return place.reshape(1, 512)

    stats = lax.all_to_all(fwd(umsg, even, odd), "item", 0, 0, tiled=True)
    own1, other1, ug1, row1, *kept = bwd(
        True, umsg, odd, ids(1), stats, positive.reshape(8, E), loss_weight.reshape(8, E)
    )
    got1 = swap(other1)
    own0, other0, ug = bwd(False, umsg, even, ids(0), *kept, ug1, row1)
    got0 = swap(other0)
    send = call(add_kernel, shape((4, CH, E), bf16), "add_cores")(own1, got1)
    ug, send = lax.optimization_barrier((ug, send))
    ug = lax.all_to_all(ug, "item", 0, 0, tiled=True)
    tall, one = shape((K * R + 8, E), f32), shape((CH, E), bf16)
    grads = (shape((R, K, E), f32), shape((K, R), f32))
    total, *sends = call(pair_kernel, (tall, one, one, one), "add_pair")(own0, got0, over_z(send, 1))
    parts = [over_z(x, m) for x, m in zip(sends, (2, 4, 6))]
    user_grad, user_gate_grad = call(users_kernel, grads, "sum_users")(ug)
    item_grad, item_gate_grad = call(items_kernel, grads, "sum_items")(total, *parts)
    return user_grad, user_gate_grad.T, item_grad, item_gate_grad.T


def solution(mesh):
    return jax.shard_map(
        shards,
        mesh=mesh,
        in_specs=(
            P(("user", "item"), None, None),
            P(("item", "user"), None, None),
            P(("user", "item"), None),
            P(("item", "user"), None),
            P("user"),
            P("user"),
        ),
        out_specs=(
            P(("user", "item"), None, None),
            P(("user", "item"), None),
            P(("item", "user"), None, None),
            P(("item", "user"), None),
        ),
        check_vma=False,
    )
```

```python
import functools
import jax
import jax.numpy as jnp
from jax import lax
from jax.experimental import pallas as pl
from jax.experimental.pallas import tpu as pltpu
from jax.sharding import PartitionSpec as P

K = 4
E = 128
R = 64
CH = K * R + 16
logit_scale = 4.0
ROWS = 512
BROWS = 512
f32 = jnp.float32
bf16 = jnp.bfloat16
VM = pl.BlockSpec(memory_space=pltpu.VMEM)


def gate_factors(msg):
    g = msg[:, K * R : K * R + 8, :].astype(f32)
    rows = [g[:, k, :] for k in range(K)]
    high = jnp.maximum(jnp.maximum(rows[0], rows[1]), jnp.maximum(rows[2], rows[3]))
    low = jnp.minimum(jnp.minimum(rows[0], rows[1]), jnp.minimum(rows[2], rows[3]))
    mid = 0.5 * (high + low) + 24.0
    return [jnp.exp(r - mid) for r in rows]


def fill_user_factors(u_ref, a_ref):
    for k, rows in enumerate(gate_factors(u_ref[...])):
        cols = rows.T
        for i in range(rows.shape[0]):
            a_ref[k, i * R : (i + 1) * R, :] = jnp.broadcast_to(cols[:R, i : i + 1], (R, E))


def fill_item_factors(i_ref, b_ref, start=0):
    for k, rows in enumerate(gate_factors(i_ref[...])):
        left = lax.broadcasted_iota(jnp.int32, (8, E), 1) < R
        for p in range(rows.shape[0] // 2):
            first = jnp.broadcast_to(rows[2 * p : 2 * p + 1, :], (8, E))
            second = jnp.broadcast_to(rows[2 * p + 1 : 2 * p + 2, :], (8, E))
            b_ref[k, :, start + p * E : start + (p + 1) * E] = jnp.where(left, first, second)


def tile2(x):
    return jnp.concatenate([x, x], axis=0)


def score_piece(u_ref, i_refs, s_ref, blk, k):
    rows = s_ref[0].shape[1]
    per = rows // R
    u = u_ref[blk * per : (blk + 1) * per, pl.ds(k * R, R), :].reshape(rows, E)
    at = 0
    for i_ref in i_refs:
        it = i_ref[:, pl.ds(k * R, R), :].reshape(-1, E)
        s = lax.dot_general(u, it, (((1,), (1,)), ((), ())), preferred_element_type=f32)
        s_ref[blk % 2][k, :, at : at + it.shape[0]] = s
        at += it.shape[0]


def inverse(x):
    return pl.reciprocal(x, approx=True)


def mixture(a, b, s):
    p = [a[k] * b[k] for k in range(K)]
    den = (p[0] + p[1]) + (p[2] + p[3])
    num = (p[0] * s[0] + p[1] * s[1]) + (p[2] * s[2] + p[3] * s[3])
    inv = inverse(den)
    return p, inv, num * inv


def fwd_kernel(u_ref, even_ref, odd_ref, out_ref, a_ref, b_ref, s0_ref, s1_ref, m_ref, t_ref):
    s_ref, i_refs = (s0_ref, s1_ref), (even_ref, odd_ref)
    n = 2 * even_ref.shape[0] * R
    users = u_ref.shape[0] * R
    blocks = users // ROWS
    fill_user_factors(u_ref, a_ref)
    for half, i_ref in enumerate(i_refs):
        fill_item_factors(i_ref, b_ref, half * n // 2)

    def first(r, _):
        score_piece(u_ref, i_refs, s_ref, 0, r)
        return 0

    lax.fori_loop(0, K, first, 0, unroll=4)
    for blk in range(blocks):

        def group(r, _, blk=blk):
            if blk + 1 < blocks:
                score_piece(u_ref, i_refs, s_ref, blk + 1, r)
            step = ROWS // (K)
            for h in range(step // 8):
                at = r * step + h * 8
                rows = pl.ds(blk * ROWS + at, 8)
                a = [a_ref[k, rows, :] for k in range(K)]
                xs = []
                for c in range(n // E):
                    lanes = slice(c * E, (c + 1) * E)
                    b = [b_ref[k, :, lanes] for k in range(K)]
                    s = [s_ref[blk % 2][k, pl.ds(at, 8), lanes] for k in range(K)]
                    xs.append(SCALE2 * mixture(a, b, s)[2])
                top = functools.reduce(jnp.maximum, xs)
                m_ref[rows, :] = top
                t_ref[rows, :] = functools.reduce(jnp.add, [EXP(x - top) for x in xs])
            return 0

        lax.fori_loop(0, K, group, 0)
    for c in range(users // E):
        top = m_ref[c * E : (c + 1) * E, :].T
        total = t_ref[c * E : (c + 1) * E, :].T
        best = jnp.max(top, axis=0, keepdims=True)
        total = jnp.sum(EXP(top - best) * total, axis=0, keepdims=True)
        for d in range(out_ref.shape[0]):
            out_ref[d, c : c + 1, :] = best
            out_ref[d, 8 + c : 9 + c, :] = total


def bwd_kernel(first, u_ref, i_ref, id_ref, *refs):
    if first:
        stat_ref, pos_ref, w_ref, own_ref, other_ref, ug_ref, row_ref, a_ref, l_ref, w4_ref, p_ref, *refs = refs
    else:
        a_ref, l_ref, w4_ref, p_ref, ug1_ref, row1_ref, own_ref, other_ref, ug_ref, row_ref, *refs = refs
    b_ref, s0_ref, s1_ref, c0_ref, c1_ref, col_ref = refs
    s_ref, c_ref = (s0_ref, s1_ref), (c0_ref, c1_ref)
    n = i_ref.shape[0] * R
    users = u_ref.shape[0] * R
    blocks = users // BROWS
    per = BROWS // R
    fill_item_factors(i_ref, b_ref)
    if first:
        fill_user_factors(u_ref, a_ref)
        tops = stat_ref[:, 0:8, :]
        top = jnp.max(tops, axis=0)
        lse = top + LOG(jnp.sum(EXP(tops - top[None]) * stat_ref[:, 8:16, :], axis=0))
        weight = logit_scale * w_ref[...]
        lse_t = (lse - LOG(weight)).T
        w_t = weight.T
        pos_t = pos_ref[...].T
        for c in range(users // E):
            at = slice(c * E, (c + 1) * E)
            l_ref[at, :] = jnp.broadcast_to(lse_t[:, c : c + 1], (E, E))
            w4_ref[at, :] = jnp.broadcast_to(w_t[:, c : c + 1], (E, E))
            p_ref[at, :] = jnp.broadcast_to(pos_t[:, c : c + 1], (E, E))
    col_ref[...] = jnp.zeros_like(col_ref)

    def gradient_piece(blk, k):
        co = c_ref[blk % 2][k]
        it = i_ref[:, pl.ds(k * R, R), :].reshape(n, E)
        u = u_ref[blk * per : (blk + 1) * per, pl.ds(k * R, R), :].reshape(BROWS, E)
        at = (slice(blk * per, (blk + 1) * per), pl.ds(k * R, R))
        ug = jnp.dot(co, it, preferred_element_type=f32).reshape(per, R, E)
        ug_ref[at] = ug if first else (ug + ug1_ref[at]).astype(bf16)
        g = lax.dot_general(co, u, (((0,), (0,)), ((), ())), preferred_element_type=f32)
        g = g.reshape(2, -1, R, E)
        for half, ref in enumerate((own_ref, other_ref)):
            if blk == 0:
                ref[:, pl.ds(k * R, R), :] = g[half]
            else:
                ref[:, pl.ds(k * R, R), :] += g[half]

    def score_only(r, _):
        score_piece(u_ref, (i_ref,), s_ref, 0, r)
        return 0

    def gradient_only(r, _):
        gradient_piece(blocks - 1, r)
        return 0

    lane = lax.broadcasted_iota(jnp.int32, (16, E), 1)
    lax.fori_loop(0, K, score_only, 0, unroll=4)
    for blk in range(blocks):

        def group(r, _, blk=blk):
            if blk + 1 < blocks:
                score_piece(u_ref, (i_ref,), s_ref, blk + 1, r)
            if blk > 0:
                gradient_piece(blk - 1, r)
            step = BROWS // K
            for h in range(step // 16):
                at = r * step + h * 16
                rows = pl.ds(blk * BROWS + at, 16)
                a = [a_ref[k, rows, :] for k in range(K)]
                lse_r, w_r, p_r = l_ref[rows, :], w4_ref[rows, :], p_ref[rows, :]
                sums = [jnp.zeros((16, E), f32) for _ in range(K - 1)]
                for c in range(n // E):
                    lanes = slice(c * E, (c + 1) * E)
                    b = [tile2(b_ref[k, :, lanes]) for k in range(K)]
                    s = [s_ref[blk % 2][k, pl.ds(at, 16), lanes] for k in range(K)]
                    p, inv, mixed = mixture(a, b, s)
                    prob = EXP(SCALE2 * mixed - lse_r)
                    hit = jnp.broadcast_to(id_ref[:, lanes], (16, E)) == p_r
                    q = jnp.where(hit, prob - w_r, prob) * inv
                    for k in range(K):
                        share = q * p[k]
                        c_ref[blk % 2][k, pl.ds(at, 16), lanes] = share.astype(bf16)
                        if k < K - 1:
                            dgate = share * (s[k] - mixed)
                            sums[k] = sums[k] + dgate
                            col_ref[k, :, lanes] += dgate[:8] + dgate[8:]
                cols = [jnp.sum(x, axis=1, keepdims=True) for x in sums]
                cols.append(-(cols[0] + cols[1] + cols[2]))
                both = jnp.where(
                    lane == 0, cols[0], jnp.where(lane == 1, cols[1], jnp.where(lane == 2, cols[2], cols[3]))
                )
                row_ref[rows, :] = both if first else both + row1_ref[rows, :]
            return 0

        for r in range(K):
            group(r, 0)
    lax.fori_loop(0, K, gradient_only, 0, unroll=4)

    if not first:
        left = lax.broadcasted_iota(jnp.int32, (8, E), 1) < R
        for c in range(users // E):
            total = row_ref[c * E : (c + 1) * E, :].T[0:8]
            high = total.astype(bf16).astype(f32)
            low = total - high
            halves = jnp.where(left, high, jnp.roll(low, R, axis=1)), jnp.where(left, jnp.roll(high, R, axis=1), low)
            for h, part in enumerate(halves):
                ug_ref[2 * c + h, K * R :, :] = jnp.concatenate([part, jnp.zeros_like(part)], axis=0).astype(bf16)
    totals = [jnp.sum(col_ref[k], axis=0, keepdims=True) for k in range(K - 1)]
    totals.append(-(totals[0] + totals[1] + totals[2]))
    for half, ref in enumerate((own_ref, other_ref)):
        ref[:, K * R :, :] = jnp.zeros((ref.shape[0], 8, E), f32)
        for k in range(K):
            for s in range(ref.shape[0] // 2):
                at = half * n // 2 + s * E
                two = totals[k][:, at : at + E]
                ref[2 * s, K * R + k : K * R + k + 1, :] = two
                ref[2 * s + 1, K * R + k : K * R + k + 1, :] = jnp.roll(two, R, axis=1)


def packed(emb_ref, gate_ref):
    emb = emb_ref[...].astype(f32)
    body = [emb[:, k, :].astype(bf16) for k in range(K)]
    gate = gate_ref[...].astype(f32)
    gate = jnp.concatenate([gate, gate], axis=1)
    gate = jnp.concatenate([gate, jnp.zeros((16 - K, E), f32)], axis=0)
    return jnp.concatenate(body + [gate.astype(bf16)], axis=0)


def pack_kernel(item_ref, igate_ref, user_ref, ugate_ref, iout_ref, uout_ref):
    iout_ref[...] = packed(item_ref, igate_ref)
    block = packed(user_ref, ugate_ref)
    for d in range(uout_ref.shape[0]):
        uout_ref[d] = block


def narrow(total):
    left = lax.broadcasted_iota(jnp.int32, (8, E), 1) < R
    gates = total[K * R :]
    high = gates.astype(bf16).astype(f32)
    both = jnp.where(left, high, jnp.roll(gates - high, R, axis=1))
    both = jnp.concatenate([both, jnp.zeros_like(both)], axis=0)
    return jnp.concatenate([total[: K * R].astype(bf16), both.astype(bf16)], axis=0)


def add_kernel(own_ref, got_ref, send_ref):
    for m in range(send_ref.shape[0]):
        send_ref[m] = narrow(own_ref[m] + got_ref[m])


def join_gates(rows):
    return rows[:8] + jnp.roll(rows[:8], R, axis=1)


def widen(part):
    part = part.astype(f32)
    return jnp.concatenate([part[: K * R], join_gates(part[K * R :])], axis=0)


def pair_kernel(own_ref, got_ref, part_ref, mine_ref, *out_refs):
    mine_ref[...] = own_ref[0] + got_ref[0] + widen(part_ref[0])
    for m, ref in enumerate(out_refs):
        ref[...] = narrow(own_ref[m + 1] + got_ref[m + 1] + widen(part_ref[m + 1]))


def items_kernel(mine_ref, a_ref, b_ref, c_ref, out_ref, gate_ref):
    total = mine_ref[...] + (widen(a_ref[...]) + widen(b_ref[...]) + widen(c_ref[...]))
    for k in range(K):
        out_ref[:, k, :] = total[k * R : (k + 1) * R]
    gate_ref[...] = total[K * R : K * R + K, :R]


def users_kernel(u_ref, out_ref, gate_ref):
    for k in range(K):
        total = u_ref[0, k * R : (k + 1) * R, :].astype(f32)
        for d in range(1, u_ref.shape[0]):
            total = total + u_ref[d, k * R : (k + 1) * R, :].astype(f32)
        out_ref[:, k, :] = total
    gates = u_ref[0, K * R :, :].astype(f32)
    for d in range(1, u_ref.shape[0]):
        gates = gates + u_ref[d, K * R :, :].astype(f32)
    gate_ref[...] = join_gates(gates)[:K, :R]


def estimate(micros):
    return pl.CostEstimate(flops=micros * 10**9, transcendentals=0, bytes_accessed=micros * 3 * 10**6)


def call(kernel, outs, name, limit=8 * 1024 * 1024):
    single = not isinstance(outs, tuple)

    def run(*args):
        return pl.pallas_call(
            kernel,
            out_shape=outs,
            in_specs=[VM] * len(args),
            out_specs=VM if single else (VM,) * len(outs),
            cost_estimate=estimate(2),
            compiler_params=pltpu.CompilerParams(vmem_limit_bytes=limit),
            name=name,
        )(*args)

    return run


EXP, LOG, SCALE2 = jnp.exp2, jnp.log2, logit_scale * 1.4426950408889634
LIMIT = 44 * 1024 * 1024
LIMIT2 = 44 * 1024 * 1024


def fwd(umsg, even, odd):
    users, n = umsg.shape[0] * R, 2 * even.shape[0] * R
    return pl.pallas_call(
        fwd_kernel,
        out_shape=jax.ShapeDtypeStruct((16, 16, E), f32),
        in_specs=[VM] * 3,
        out_specs=VM,
        scratch_shapes=[
            pltpu.VMEM((K, users, E), f32),
            pltpu.VMEM((K, 8, n), f32),
            pltpu.VMEM((K, ROWS, n), f32),
            pltpu.VMEM((K, ROWS, n), f32),
            pltpu.VMEM((users, E), f32),
            pltpu.VMEM((users, E), f32),
        ],
        compiler_params=pltpu.CompilerParams(vmem_limit_bytes=LIMIT),
        cost_estimate=estimate(6),
        name="score_stats",
    )(umsg, even, odd)


def bwd(first, umsg, imsg, ids, *more):
    users, n = umsg.shape[0] * R, imsg.shape[0] * R
    shape = jax.ShapeDtypeStruct
    part = shape((imsg.shape[0] // 2, K * R + 8, E), f32)
    column = shape((users, E), f32)
    outs = [part, part]
    if first:
        outs += [shape((users // R, K * R, E), f32), column, shape((K, users, E), f32)]
        outs += [column, column, shape((users, E), jnp.int32)]
    else:
        outs += [shape(umsg.shape, bf16)]
    return pl.pallas_call(
        functools.partial(bwd_kernel, first),
        out_shape=tuple(outs),
        in_specs=[VM] * (3 + len(more)),
        out_specs=(VM,) * len(outs),
        scratch_shapes=([] if first else [pltpu.VMEM((users, E), f32)])
        + [
            pltpu.VMEM((K, 8, n), f32),
            pltpu.VMEM((K, BROWS, n), f32),
            pltpu.VMEM((K, BROWS, n), f32),
            pltpu.VMEM((K, BROWS, n), bf16),
            pltpu.VMEM((K, BROWS, n), bf16),
            pltpu.VMEM((K, 8, n), f32),
        ],
        compiler_params=pltpu.CompilerParams(vmem_limit_bytes=LIMIT2),
        cost_estimate=estimate(8),
        name="gradients_odd" if first else "gradients_even",
    )(umsg, imsg, ids, *more)


def shards(user_emb, item_emb, user_gate, item_gate, positive, loss_weight):
    index = lax.axis_index("user")
    z, core = index // 2, index % 2
    shape = jax.ShapeDtypeStruct

    def over_z(x, mask):
        return lax.ppermute(x, "user", [(2 * a + c, 2 * (a ^ mask) + c) for a in range(8) for c in range(2)])

    def swap(x):
        return lax.ppermute(x, "user", [(a, a ^ 1) for a in range(16)])

    packs = (shape((CH, E), bf16), shape((16, CH, E), bf16))
    mine, umsg = call(pack_kernel, packs, "pack", 60 * 1024 * 1024)(item_emb, item_gate.T, user_emb, user_gate.T)
    umsg = lax.all_to_all(umsg, "item", 0, 0, tiled=True)
    far = over_z(mine, 4)
    mine, far = lax.optimization_barrier((mine, far))
    even = jnp.stack([mine, over_z(mine, 2), far, over_z(mine, 6)])
    odd = over_z(even, 1)
    even = jnp.concatenate([even, swap(even)], axis=0)
    odd = jnp.concatenate([odd, swap(odd)], axis=0)
    slot = jnp.arange(8, dtype=jnp.int32)

    def ids(parity):
        place = 2 * (z ^ (2 * (slot % 4) + parity)) + (core ^ (slot // 4))
        place = lax.axis_index("item") * 1024 + place[:, None] * R + jnp.arange(R, dtype=jnp.int32)[None]
        return place.reshape(1, 512)

    stats = lax.all_to_all(fwd(umsg, even, odd), "item", 0, 0, tiled=True)
    own1, other1, ug1, row1, *kept = bwd(
        True, umsg, odd, ids(1), stats, positive.reshape(8, E), loss_weight.reshape(8, E)
    )
    got1 = swap(other1)
    own0, other0, ug = bwd(False, umsg, even, ids(0), *kept, ug1, row1)
    got0 = swap(other0)
    send = call(add_kernel, shape((4, CH, E), bf16), "add_cores")(own1, got1)
    ug, send = lax.optimization_barrier((ug, send))
    ug = lax.all_to_all(ug, "item", 0, 0, tiled=True)
    tall, one = shape((K * R + 8, E), f32), shape((CH, E), bf16)
    grads = (shape((R, K, E), f32), shape((K, R), f32))
    total, *sends = call(pair_kernel, (tall, one, one, one), "add_pair")(own0, got0, over_z(send, 1))
    parts = [over_z(x, m) for x, m in zip(sends, (2, 4, 6))]
    user_grad, user_gate_grad = call(users_kernel, grads, "sum_users")(ug)
    item_grad, item_gate_grad = call(items_kernel, grads, "sum_items")(total, *parts)
    return user_grad, user_gate_grad.T, item_grad, item_gate_grad.T


def solution(mesh):
    return jax.shard_map(
        shards,
        mesh=mesh,
        in_specs=(
            P(("user", "item"), None, None),
            P(("item", "user"), None, None),
            P(("user", "item"), None),
            P(("item", "user"), None),
            P("user"),
            P("user"),
        ),
        out_specs=(
            P(("user", "item"), None, None),
            P(("user", "item"), None),
            P(("item", "user"), None, None),
            P(("item", "user"), None),
        ),
        check_vma=False,
    )
```
